32 devices in a mesh: groups: 2 (over x), dp: 8 (over z, y), tensor: 2 (over core).
Axes of the slice: x: 2, y: 2, z: 4, core: 2. Of those that a mesh axis runs over, the one named last changes fastest.
Arguments:
- queries: bfloat16 [128, 8, 8192], P(('groups', 'dp'), None, 'tensor'), parts along dimension 0, may hold values from -200 to 200
- cache_keys: bfloat16 [128, 96, 1024], P(('groups', 'dp'), None, 'tensor'), parts along dimension 0, may hold values from -6 to 6
- cache_values: bfloat16 [128, 96, 1024], P(('groups', 'dp'), None, 'tensor'), parts along dimension 0, may hold values from -6 to 6
- new_keys: bfloat16 [128, 8, 1024], P(('groups', 'dp'), None, 'tensor'), parts along dimension 0, may hold values from -6 to 6
- new_values: bfloat16 [128, 8, 1024], P(('groups', 'dp'), None, 'tensor'), parts along dimension 0, may hold values from -6 to 6
- features: bfloat16 [128, 104, 5120], P(('groups', 'dp')), parts along dimension 0, may hold values from -6 to 6
- cotangent: bfloat16 [128, 8, 8192], P(('groups', 'dp'), None, 'tensor'), parts along dimension 0, may hold values from -6 to 6
- rewards: float32 [128], P(('groups', 'dp')), parts along dimension 0, may hold values from 0 to 4
- lengths: int32 [128], P(('groups', 'dp')), parts along dimension 0, may hold values from 1 to 96, 3072 in all
Outputs:
- attended: bfloat16 [128, 8, 8192], P(('groups', 'dp'), None, 'tensor'), parts along dimension 0
- value_grad: float32 [10240, 1024], P(('groups', 'dp'), 'tensor'), parts along dimension 0
- bucket_peaks: float32 [16], P(('groups', 'tensor')), parts along dimension 0
The draws below stay inside these ranges and needn't reach their ends.
There are 2 independent parts, one for each index of `groups`. The reference program is written for one: setup_inputs(seed, part) draws one part's arguments, and reference() takes and returns one part's arrays. A program takes and returns all parts, laid end to end along the dimension named above; each array names one. Nothing has to cross between parts.
Inputs may be any that keep to these rules, and one draw needn't show every extreme that they name: lengths of one part sum to half of 64 times 96, and some rollout has length 96.
All inputs are finite; a program needn't handle non-finite values. No bound on the sum of `lengths` on one device may be relied on, other than what follows from the above.
Results may differ from the reference program's by a relative error of at most 0.0057.
Values sent between devices are 32-bit elements; how exact they have to be, the bound alone decides.
No kernel may reach another device: no remote copies, remote signals or barrier semaphores. Data moves between devices by JAX's collectives and lax.ppermute only.
A program may use at most 64 MiB of HBM per device.

```python
import math
import jax
import jax.numpy as jnp
import numpy as np
from jax import lax

D = 5120
H = 64
KVH = 8
HD = 128
GROUP = 8
STEPS = 8
CTX = 96
BUCKET = 128
ROLLOUTS = 64


def shared_keys(key):
    return jnp.clip(jax.random.normal(key, (ROLLOUTS, CTX, KVH * HD), jnp.float32), -6.0, 6.0)


def draw_cache_keys(key, part):
    base_keys = shared_keys(key)
    return base_keys.astype(jnp.bfloat16)


def draw_queries(key, part):
    key = jax.random.fold_in(key, 23)
    fresh_rows = jnp.clip(jax.random.normal(key, (ROLLOUTS, STEPS, H * HD), jnp.float32), -6.0, 6.0)
    return fresh_rows.astype(jnp.bfloat16)


def level_of(stream_key, dims, cuts, low, high):
    gain = 1.0
    for dim, blocks in cuts:
        steps = jax.random.uniform(jax.random.fold_in(jax.random.fold_in(stream_key, 6), dim), (blocks,), jnp.float32, low / len(cuts), high / len(cuts))
        gain = gain * jnp.repeat(jnp.exp(steps), dims[dim] // blocks).reshape((-1,) + (1,) * (len(dims) - 1 - dim))
    return gain


def split_up(count, total, reach, skew):
    loads = [(1 << 20) // math.isqrt(grade ** skew) + 1 for grade in range(2, count + 1)]
    surplus, given = total - reach - (count - 1), [1] * (count - 1)
    while surplus > 0:
        free = [i for i in range(count - 1) if given[i] < reach]
        whole, left = sum([loads[i] for i in free]), surplus
        for i in free:
            addition = min(reach - given[i], max(1, left * loads[i] // whole), surplus)
            given[i] = given[i] + addition
            surplus = surplus - addition
    return np.array([reach] + given)


def uneven(rng, amount, total, reach, skew):
    if amount == 2:
        one = jax.random.randint(rng, (), max(1, total - reach), min(reach, total - 1) + 1)
        return jnp.stack([one, total - one])
    tallies = jnp.asarray(split_up(amount, total, reach, skew), jnp.int32)
    twos = (amount - 1) // 2
    giver, sink = tallies[1:1 + 2 * twos:2], tallies[2:2 + 2 * twos:2]
    margin = jnp.minimum(giver - 1, reach - sink)
    shifted = jax.random.randint(jax.random.fold_in(rng, 1), (twos,), 0, 1 << 20) % (margin + 1)
    tallies = tallies.at[1:1 + 2 * twos:2].set(giver - shifted).at[2:2 + 2 * twos:2].set(sink + shifted)
    return tallies[jax.random.permutation(jax.random.fold_in(rng, 2), amount)]


def normal_values(stream_key, dims, width, bound, cuts=(), dtype=jnp.bfloat16):
    array = jax.random.normal(stream_key, dims, jnp.float32) * width
    if len(cuts) > 0:
        array = level_of(stream_key, dims, cuts, -0.22, 0.18) * array
    return jnp.clip(array, min=-bound, max=bound).astype(dtype)


def setup_inputs(seed: int = 0, part: int = 0) -> dict:
    keys = jax.random.split(jax.random.key(seed), 10)
    part_splits = jax.random.split(jax.random.fold_in(keys[9], part), 10)
    return {
        "queries": draw_queries(jax.random.fold_in(jax.random.fold_in(keys[9], part), 71), part),
        "cache_keys": draw_cache_keys(jax.random.fold_in(jax.random.fold_in(keys[9], part), 71), part),
        "cache_values": normal_values(part_splits[2], (ROLLOUTS, CTX, KVH * HD), 1.0, 6.0, ((0, 8), (2, 2))),
        "new_keys": normal_values(part_splits[3], (ROLLOUTS, STEPS, KVH * HD), 1.0, 6.0, ((0, 8), (2, 2))),
        "new_values": normal_values(part_splits[4], (ROLLOUTS, STEPS, KVH * HD), 1.0, 6.0, ((0, 8), (2, 2))),
        "features": normal_values(part_splits[5], (ROLLOUTS, CTX + STEPS, D), 1.0, 6.0, ((0, 8),)),
        "cotangent": normal_values(part_splits[6], (ROLLOUTS, STEPS, H * HD), 1.0, 6.0, ((0, 8), (2, 2))),
        "rewards": jnp.clip(4.0 * jax.random.uniform(part_splits[7], (ROLLOUTS,), jnp.float32) ** level_of(part_splits[7], (ROLLOUTS,), ((0, 8),), -0.2, 0.2), 0.0, 4.0),
        "lengths": uneven(part_splits[8], ROLLOUTS, ROLLOUTS * CTX // 2, CTX, 2).astype(jnp.int32),
    }


def attend_rollout(queries_one, past_keys, past_values, fresh_keys, fresh_values, cot_one, live_count, advantage_one):
    step_count = queries_one.shape[0]
    group_count = past_keys.shape[-1] // HD
    head_count = queries_one.shape[-1] // HD
    grouped = queries_one.astype(jnp.float32).reshape(step_count, group_count, head_count // group_count, HD)
    keys_past = past_keys.astype(jnp.float32).reshape(-1, group_count, HD)
    values_past = past_values.astype(jnp.float32).reshape(-1, group_count, HD)
    keys_new = fresh_keys.astype(jnp.float32).reshape(step_count, group_count, HD)
    values_new = fresh_values.astype(jnp.float32).reshape(step_count, group_count, HD)
    scaling = 1.0 / math.sqrt(HD)
    scores_past = jnp.einsum('sgjd,cgd->sgjc', grouped, keys_past) * scaling
    scores_new = jnp.einsum('sgjd,tgd->sgjt', grouped, keys_new) * scaling
    filled = jnp.arange(keys_past.shape[0])[None, None, None, :] < live_count
    scores_past = jnp.where(filled, scores_past, -1e+30)
    causal = jnp.arange(step_count)[:, None, None, None] >= jnp.arange(step_count)[None, None, None, :]
    scores_new = jnp.where(causal, scores_new, -1e+30)
    highest = jnp.maximum(lax.optimization_barrier(jnp.max(scores_past, axis=-1)), lax.optimization_barrier(jnp.max(scores_new, axis=-1)))[..., None]
    lift_past = jnp.exp(scores_past - highest)
    lift_new = jnp.exp(scores_new - highest)
    totals = lax.optimization_barrier(jnp.sum(lift_past, axis=-1, keepdims=True)) + lax.optimization_barrier(jnp.sum(lift_new, axis=-1, keepdims=True))
    weight_past = (lift_past / totals).astype(jnp.bfloat16).astype(jnp.float32)
    weight_new = (lift_new / totals).astype(jnp.bfloat16).astype(jnp.float32)
    result = jnp.einsum('sgjc,cgd->sgjd', weight_past, values_past) + jnp.einsum('sgjt,tgd->sgjd', weight_new, values_new)
    scaled = (cot_one.astype(jnp.float32) * advantage_one).astype(jnp.bfloat16).astype(jnp.float32)
    scaled = scaled.reshape(step_count, group_count, head_count // group_count, HD)
    cot_past = jnp.einsum('sgjc,sgjd->cgd', weight_past, scaled).reshape(-1, group_count * HD)
    cot_new = jnp.einsum('sgjt,sgjd->tgd', weight_new, scaled).reshape(step_count, group_count * HD)
    value_cot = jnp.concatenate([cot_past, cot_new], axis=0).astype(jnp.bfloat16)
    return (result.reshape(step_count, head_count * HD).astype(jnp.bfloat16), value_cot)

def reference(queries, cache_keys, cache_values, new_keys, new_values, features, cotangent, rewards, lengths):
    grouped_rewards = rewards.reshape(-1, GROUP)
    centre = lax.optimization_barrier(jnp.mean(grouped_rewards, axis=1, keepdims=True))
    spread = jnp.sqrt(lax.optimization_barrier(jnp.mean((grouped_rewards - centre) ** 2, axis=1, keepdims=True)))
    advantage = ((grouped_rewards - centre) / jnp.maximum(spread, 1.0)).reshape(-1)
    attended, value_cot = lax.map(lambda items: attend_rollout(*items), (queries, cache_keys, cache_values, new_keys, new_values, cotangent, lengths, advantage))
    value_grad = jnp.dot(features.reshape(-1, D).T, value_cot.reshape(-1, KVH * HD), preferred_element_type=jnp.float32)
    bucket_peaks = lax.optimization_barrier(jnp.max(jnp.abs(value_grad).reshape(D, KVH * HD // BUCKET, BUCKET), axis=(0, 2)))
    return (attended, value_grad, bucket_peaks)
```

```python
import functools
import math

import jax
import jax.numpy as jnp
from jax import lax
from jax.experimental import pallas as pl
from jax.experimental.pallas import tpu as pltpu
from jax.sharding import PartitionSpec as P

HD = 128
GROUP = 8
BUCKET = 128
VMEM_BYTES = 40 * 1024 * 1024


def attend_kernel(lengths, rewards, q, ck, cv, nk, nv, cot, *rest):
    out, cot_t, rows = rest[-3:]
    rollouts, steps, width = q.shape
    heads = width // HD
    ctx = ck.shape[1]
    slots = ctx + steps
    padded = -(-slots // HD) * HD
    pad = padded - slots
    scaling = 1.0 / math.sqrt(HD)

    def by_head(block):
        return jnp.concatenate(
            [block[:, j * HD : (j + 1) * HD].astype(jnp.float32) for j in range(heads)], axis=0
        )

    def joined(past, fresh):
        fresh = jnp.concatenate(
            [fresh.astype(jnp.float32), jnp.zeros((pad, HD), jnp.float32)], axis=0
        ).astype(jnp.bfloat16)
        return jnp.concatenate([past, fresh], axis=0)

    shape = (heads * steps, padded)
    column = lax.broadcasted_iota(jnp.int32, shape, 1)
    step = lax.broadcasted_iota(jnp.int32, shape, 0) % steps
    fresh_live = (column >= ctx) & (column - ctx <= step)
    for base in range(0, rollouts, GROUP):
        centre = rewards[base]
        for i in range(1, GROUP):
            centre = centre + rewards[base + i]
        centre = centre * (1.0 / GROUP)
        spread = (rewards[base] - centre) * (rewards[base] - centre)
        for i in range(1, GROUP):
            spread = spread + (rewards[base + i] - centre) * (rewards[base + i] - centre)
        spread = jnp.sqrt(jnp.full((1, HD), spread * (1.0 / GROUP), jnp.float32))
        spread = jnp.maximum(spread, 1.0)
        for r in range(base, base + GROUP):
            advantage = jnp.full((1, HD), rewards[r] - centre, jnp.float32) / spread
            keys = joined(ck[r], nk[r])
            values = joined(cv[r], nv[r])
            scores = lax.dot_general(
                by_head(q[r]).astype(jnp.bfloat16),
                keys,
                (((1,), (1,)), ((), ())),
                preferred_element_type=jnp.float32,
            )
            scores = scores * scaling
            scores = jnp.where((column < lengths[r]) | fresh_live, scores, -1e30)
            highest = jnp.max(scores, axis=1, keepdims=True)
            lift = jnp.exp(scores - highest)
            weights = (lift / jnp.sum(lift, axis=1, keepdims=True)).astype(jnp.bfloat16)
            result = jnp.dot(weights, values, preferred_element_type=jnp.float32)
            for j in range(heads):
                out[r, :, j * HD : (j + 1) * HD] = result[j * steps : (j + 1) * steps].astype(
                    jnp.bfloat16
                )
            scaled = (by_head(cot[r]) * advantage).astype(jnp.bfloat16)
            value_cot = lax.dot_general(
                weights, scaled, (((0,), (0,)), ((), ())), preferred_element_type=jnp.float32
            )
            rows[r * slots : (r + 1) * slots, :] = value_cot[:slots]
    cot_t[...] = rows[...].T.astype(jnp.bfloat16)


def attend(g, lengths, rewards, queries, ck, cv, nk, nv, cotangent, attended):
    rollouts, steps, width = queries.shape
    ctx = ck.shape[1]
    key_heads = ck.shape[2] // HD
    wide = width // key_heads
    slots = rollouts * (ctx + steps)

    def block(dims):
        return pl.BlockSpec(dims, lambda i: (0, 0, g))

    smem = pl.BlockSpec(memory_space=pltpu.SMEM)
    in_specs = [
        smem,
        smem,
        block((rollouts, steps, wide)),
        block((rollouts, ctx, HD)),
        block((rollouts, ctx, HD)),
        block((rollouts, steps, HD)),
        block((rollouts, steps, HD)),
        block((rollouts, steps, wide)),
    ]
    args = [lengths, rewards, queries, ck, cv, nk, nv, cotangent]
    aliases = {}
    if attended is not None:
        in_specs.append(pl.BlockSpec(memory_space=pl.ANY))
        args.append(attended)
        aliases = {8: 0}
    return pl.pallas_call(
        attend_kernel,
        grid=(1,),
        in_specs=in_specs,
        out_specs=[
            block((rollouts, steps, wide)),
            pl.BlockSpec((HD, slots), lambda i: (0, 0)),
        ],
        out_shape=[
            jax.ShapeDtypeStruct(queries.shape, jnp.bfloat16),
            jax.ShapeDtypeStruct((HD, slots), jnp.bfloat16),
        ],
        scratch_shapes=[pltpu.VMEM((slots, HD), jnp.float32)],
        input_output_aliases=aliases,
        compiler_params=pltpu.CompilerParams(vmem_limit_bytes=VMEM_BYTES),
        cost_estimate=pl.CostEstimate(
            flops=6 * rollouts * steps * wide * HD,
            bytes_accessed=rollouts * (3 * steps * wide + 2 * ctx * HD) * 2,
            transcendentals=rollouts * steps * wide,
        ),
        name="attend",
    )(*args)


def chunk_kernel(where, features, *refs):
    count = len(refs) // 2
    left = jnp.concatenate([ref[...] for ref in refs[:count]], axis=0)
    result = jnp.dot(left, features[...], preferred_element_type=jnp.float32)
    for i in range(count):
        refs[count + i][...] = result[i * BUCKET : (i + 1) * BUCKET]


def chunks(where, slot, features, cots, width):
    depth = features.shape[0]
    count = len(cots)
    return pl.pallas_call(
        chunk_kernel,
        grid_spec=pltpu.PrefetchScalarGridSpec(
            num_scalar_prefetch=1,
            grid=(1,),
            in_specs=[pl.BlockSpec((depth, width), lambda i, where: (0, where[slot]))]
            + [pl.BlockSpec((BUCKET, depth), lambda i, where: (0, 0))] * count,
            out_specs=[pl.BlockSpec((BUCKET, width), lambda i, where: (0, 0))] * count,
        ),
        out_shape=[jax.ShapeDtypeStruct((BUCKET, width), jnp.float32)] * count,
        compiler_params=pltpu.CompilerParams(vmem_limit_bytes=VMEM_BYTES),
        cost_estimate=pl.CostEstimate(
            flops=2 * depth * width * BUCKET * count,
            bytes_accessed=2 * depth * (width + BUCKET * count) + 4 * BUCKET * width * count,
            transcendentals=0,
        ),
        name="chunk",
    )(where, features, *cots)


def finish_kernel(bucket, count, *refs):
    total = refs[0][...]
    for ref in refs[1:count]:
        total = total + ref[...]
    grad, peaks = refs[-2:]
    grad[...] = total.T
    peak = jnp.max(jnp.max(jnp.abs(total), axis=0, keepdims=True), axis=1, keepdims=True)
    peak = jnp.broadcast_to(peak, peaks.shape)
    if len(refs) > count + 2:
        lane = lax.broadcasted_iota(jnp.int32, peaks.shape, 1)
        peak = jnp.where(lane == bucket, peak, refs[count + 1][...])
    peaks[...] = peak


def finish(bucket, parts, grad, peaks, columns):
    width = parts[0].shape[1]
    count = len(parts)
    whole = pl.BlockSpec((BUCKET, width), lambda i: (0, 0))
    tile = pl.BlockSpec((8, 128), lambda i: (0, 0))
    in_specs = [whole] * count
    args = list(parts)
    aliases = {}
    if grad is not None:
        in_specs += [pl.BlockSpec(memory_space=pl.ANY), tile]
        args += [grad, peaks]
        aliases = {count: 0}
    return pl.pallas_call(
        functools.partial(finish_kernel, bucket, count),
        grid=(1,),
        in_specs=in_specs,
        out_specs=[pl.BlockSpec((width, BUCKET), lambda i: (0, bucket)), tile],
        out_shape=[
            jax.ShapeDtypeStruct((width, columns), jnp.float32),
            jax.ShapeDtypeStruct((8, 128), jnp.float32),
        ],
        input_output_aliases=aliases,
        compiler_params=pltpu.CompilerParams(vmem_limit_bytes=VMEM_BYTES),
        name="finish",
    )(*args)


def reduce_on_grid(features, cots, dp):
    width = features.shape[1] // dp
    rank = lax.axis_index("dp")
    edge = (rank < 2) | (rank >= 6)

    table = []
    for r in range(dp):
        z, y = r // 2, r % 2
        planes = [3, 2] if z < 2 else [0, 1]
        planes += [z ^ 1, z]
        table.append([p * 2 + 1 - y for p in planes] + [p * 2 + y for p in planes])
    where = jnp.asarray(table, jnp.int32)[rank]

    def across(x):
        return lax.ppermute(x, "dp", [(r, r ^ 1) for r in range(dp)])

    def pair(x):
        return lax.ppermute(x, "dp", [(r, r ^ 2) for r in range(dp)])

    def outward(x):
        return lax.ppermute(x, "dp", [(r, r ^ 2) for r in (0, 1, 6, 7)])

    def middle(x):
        return lax.ppermute(x, "dp", [(r, r ^ 6) for r in (2, 3, 4, 5)])

    count = len(cots)
    first = {}
    for s in range(0, count, 2):
        first[s] = chunks(where, 0, features, [cots[s]], width)[0]
        first[s + 1] = chunks(where, 2, features, [cots[s + 1]], width)[0]
    own3 = chunks(where, 4, features, cots, width)
    cross3 = chunks(where, 0, features, cots[1::2], width)
    cross2 = chunks(where, 1, features, cots, width)
    own2 = chunks(where, 5, features, cots, width)
    crossp = chunks(where, 2, features, cots[0::2], width)
    ownp = chunks(where, 6, features, cots, width)
    crosso = chunks(where, 3, features, cots, width)
    owno = chunks(where, 7, features, cots, width)

    streams = []
    for s in range(0, count, 2):
        streams.append({"a": s, "b": s + 1, "half": s // 2})
    y, e, m = {}, {}, {}
    for t in range(7):
        for s in streams:
            a, b, h = s["a"], s["b"], s["half"]
            k = (h, t)
            send = [first[a], cross3[h], cross2[a], cross2[b], crossp[h], crosso[a], None][t]
            if t == 6:
                send = crosso[b] + e[h, 0]
            y[k] = across(send)
            if t == 0:
                e[k] = pair(first[b])
            elif t == 1:
                e[k] = outward(own3[a] + y[h, 0])
            elif t == 2:
                e[k] = outward(own3[b] + y[h, 1])
            elif t == 3:
                e[k] = outward(own2[a] + y[h, 2])
            elif t == 4:
                e[k] = pair(jnp.where(edge, own2[b] + y[h, 3], ownp[b] + m[h, 3]))
            elif t == 5:
                e[k] = pair(ownp[a] + y[h, 4] + m[h, 2])
            else:
                e[k] = outward(ownp[b])
            if t == 2:
                m[k] = middle(own3[a] + y[h, 0] + e[h, 1])
            elif t == 3:
                m[k] = middle(own3[b] + y[h, 1] + e[h, 2])
            elif t == 4:
                m[k] = middle(own2[a] + y[h, 2] + e[h, 3])
            elif t == 5:
                m[k] = middle(own2[b] + y[h, 3] + e[h, 4])
    grad = peaks = None
    for s in streams:
        a, h = s["a"], s["half"]
        grad, peaks = finish(
            a, [owno[a], y[h, 5], e[h, 5], m[h, 4]], grad, peaks, count * BUCKET
        )
    for s in streams:
        b, h = s["b"], s["half"]
        early = jnp.where(edge, e[h, 4], 0.0)
        grad, peaks = finish(
            b, [owno[b] + early, y[h, 6], e[h, 6], m[h, 5]], grad, peaks, count * BUCKET
        )
    for hop in (1, 2, 4):
        peaks = jnp.maximum(
            peaks, lax.ppermute(peaks, "dp", [(r, r ^ hop) for r in range(dp)])
        )
    return grad, peaks[0, :count]


def reduce_plain(features, cots):
    partial_grad = lax.dot_general(
        features,
        jnp.concatenate(cots, axis=0),
        (((0,), (1,)), ((), ())),
        preferred_element_type=jnp.float32,
    )
    grad = lax.psum_scatter(partial_grad, "dp", scatter_dimension=0, tiled=True)
    peaks = jnp.max(jnp.abs(grad).reshape(-1, len(cots), BUCKET), axis=(0, 2))
    return grad, lax.pmax(peaks, "dp")


def per_device(
    dp,
    queries,
    cache_keys,
    cache_values,
    new_keys,
    new_values,
    features,
    cotangent,
    rewards,
    lengths,
):
    key_heads = cache_keys.shape[2] // HD
    attended, cots = None, []
    for g in range(key_heads):
        attended, cot = attend(
            g,
            lengths,
            rewards,
            queries,
            cache_keys,
            cache_values,
            new_keys,
            new_values,
            cotangent,
            attended,
        )
        cots.append(cot)
    flat = features.reshape(-1, features.shape[2])
    if dp == 8 and key_heads % 2 == 0 and features.shape[2] % (8 * BUCKET) == 0:
        grad, peaks = reduce_on_grid(flat, cots, dp)
    else:
        grad, peaks = reduce_plain(flat, cots)
    return attended, grad, peaks


def solution(mesh):
    split = P(("groups", "dp"), None, "tensor")
    rows = P(("groups", "dp"))
    in_specs = (
        split,
        split,
        split,
        split,
        split,
        P(("groups", "dp"), None, None),
        split,
        rows,
        rows,
    )
    out_specs = (split, P(("groups", "dp"), "tensor"), P(("groups", "tensor")))
    return jax.shard_map(
        functools.partial(per_device, mesh.shape["dp"]),
        mesh=mesh,
        in_specs=in_specs,
        out_specs=out_specs,
        check_vma=False,
    )
```

```python
import functools
import math

import jax
import jax.numpy as jnp
from jax import lax
from jax.experimental import pallas as pl
from jax.experimental.pallas import tpu as pltpu
from jax.sharding import PartitionSpec as P

HD = 128
GROUP = 8
BUCKET = 128
BATCH = 16
VMEM_BYTES = 60 * 1024 * 1024
HBM = pl.BlockSpec(memory_space=pltpu.HBM)
PARAMS = pltpu.CompilerParams(vmem_limit_bytes=VMEM_BYTES)
FAR3, FAR2, PAIR, OWN = range(4)
CROSS, SAME = True, False


def attend_heads(lengths, rewards, q, ck, cv, nk, nv, cot, out, rows):
    rollouts, steps, width = q.shape
    key_heads = ck.shape[2] // HD
    heads = width // HD // key_heads
    ctx = ck.shape[1]
    slots = ctx + steps
    padded = -(-slots // HD) * HD
    pad = padded - slots
    scaling = 1.0 / math.sqrt(HD)

    def by_head(ref, r, g):
        return jnp.concatenate(
            [
                ref[r, :, (g * heads + j) * HD : (g * heads + j + 1) * HD].astype(jnp.float32)
                for j in range(heads)
            ],
            axis=0,
        )

    def joined(past, fresh, r, g):
        lanes = slice(g * HD, (g + 1) * HD)
        fresh = jnp.concatenate(
            [fresh[r, :, lanes].astype(jnp.float32), jnp.zeros((pad, HD), jnp.float32)], axis=0
        ).astype(jnp.bfloat16)
        return jnp.concatenate([past[r, :, lanes], fresh], axis=0)

    shape = (heads * steps, padded)
    column = lax.broadcasted_iota(jnp.int32, shape, 1)
    step = lax.broadcasted_iota(jnp.int32, shape, 0) % steps
    fresh_live = (column >= ctx) & (column - ctx <= step)
    advantages, lives = [], []
    for base in range(0, rollouts, GROUP):
        centre = rewards[base]
        for i in range(1, GROUP):
            centre = centre + rewards[base + i]
        centre = centre * (1.0 / GROUP)
        spread = (rewards[base] - centre) * (rewards[base] - centre)
        for i in range(1, GROUP):
            spread = spread + (rewards[base + i] - centre) * (rewards[base + i] - centre)
        spread = jnp.sqrt(jnp.full((1, HD), spread * (1.0 / GROUP), jnp.float32))
        spread = jnp.maximum(spread, 1.0)
        for r in range(base, base + GROUP):
            advantages.append(jnp.full((1, HD), rewards[r] - centre, jnp.float32) / spread)
    for r in range(rollouts):
        lives.append((column < lengths[r]) | fresh_live)
    units = [(r, g) for g in range(key_heads) for r in range(rollouts)]
    for start in range(0, len(units), BATCH):
        batch = units[start : start + BATCH]
        scores = [
            lax.dot_general(
                by_head(q, r, g).astype(jnp.bfloat16),
                joined(ck, nk, r, g),
                (((1,), (1,)), ((), ())),
                preferred_element_type=jnp.float32,
            )
            for r, g in batch
        ]
        scores = [
            jnp.where(lives[r], x * scaling, -1e30) for (r, g), x in zip(batch, scores)
        ]
        highest = [jnp.max(x, axis=1, keepdims=True) for x in scores]
        lift = [jnp.exp(x - top) for x, top in zip(scores, highest)]
        totals = [jnp.sum(x, axis=1, keepdims=True) for x in lift]
        weights = [(x / total).astype(jnp.bfloat16) for x, total in zip(lift, totals)]
        results = [
            jnp.dot(w, joined(cv, nv, r, g), preferred_element_type=jnp.float32)
            for (r, g), w in zip(batch, weights)
        ]
        value_cots = [
            lax.dot_general(
                w,
                (by_head(cot, r, g) * advantages[r]).astype(jnp.bfloat16),
                (((0,), (0,)), ((), ())),
                preferred_element_type=jnp.float32,
            )
            for (r, g), w in zip(batch, weights)
        ]
        for (r, g), result, value_cot in zip(batch, results, value_cots):
            for j in range(heads):
                out[r, :, (g * heads + j) * HD : (g * heads + j + 1) * HD] = result[
                    j * steps : (j + 1) * steps
                ].astype(jnp.bfloat16)
            rows[r * slots : (r + 1) * slots, g * HD : (g + 1) * HD] = value_cot[:slots]


def block_of(kind):
    plane_kind, cross = kind
    rank = lax.axis_index("dp")
    plane = rank // 2
    row = rank - plane * 2
    low = plane < 2
    if plane_kind == FAR3:
        target = jnp.where(low, 3, 0)
    elif plane_kind == FAR2:
        target = jnp.where(low, 2, 1)
    elif plane_kind == PAIR:
        target = plane + 1 - 2 * (plane - (plane // 2) * 2)
    else:
        target = plane
    return target * 2 + (1 - row if cross else row)


def start_features(features, kinds, buffers, sems):
    copies = []
    for i, kind in enumerate(kinds):
        width = buffers.shape[2]
        first = pl.multiple_of(block_of(kind) * width, HD)
        copy = pltpu.make_async_copy(
            features.at[:, pl.ds(first, width)], buffers.at[i], sems.at[i]
        )
        copy.start()
        copies.append(copy)
    return copies


def begin_kernel(kinds, *refs):
    ins, refs = refs[:8], refs[8:]
    features, refs = refs[0], refs[1:]
    out, halves, refs = refs[0], refs[1:3], refs[3:]
    firsts, refs = refs[: len(kinds)], refs[len(kinds) :]
    bufs, (rows, blocks, sems, block_sems) = refs[:8], refs[8:]
    copies = []
    for i in range(8):
        copy = pltpu.make_async_copy(ins[i], bufs[i], sems.at[i])
        copy.start()
        copies.append(copy)
    block_copies = start_features(features, kinds, blocks, block_sems)
    for copy in copies:
        copy.wait()
    attend_heads(*bufs, out, rows)
    cots = rows[...].T.astype(jnp.bfloat16)
    half = cots.shape[0] // 2
    halves[0][...] = cots[:half]
    halves[1][...] = cots[half:]
    for i in range(len(kinds)):
        block_copies[i].wait()
        firsts[i][...] = jnp.dot(cots[:half], blocks[i], preferred_element_type=jnp.float32)


def begin(arrays, features, kinds, width):
    lengths, rewards, queries, ck = arrays[:4]
    depth = features.shape[0]
    columns = ck.shape[2]
    half = columns // 2
    shapes = (
        [jax.ShapeDtypeStruct(queries.shape, jnp.bfloat16)]
        + [jax.ShapeDtypeStruct((half, depth), jnp.bfloat16)] * 2
        + [jax.ShapeDtypeStruct((half, width), jnp.float32)] * len(kinds)
    )
    return pl.pallas_call(
        functools.partial(begin_kernel, kinds),
        in_specs=[HBM] * 9,
        out_specs=[pl.BlockSpec(memory_space=pltpu.VMEM)] * len(shapes),
        out_shape=shapes,
        scratch_shapes=[pltpu.SMEM(x.shape, x.dtype) for x in arrays[:2]]
        + [pltpu.VMEM(x.shape, x.dtype) for x in arrays[2:]]
        + [
            pltpu.VMEM((depth, columns), jnp.float32),
            pltpu.VMEM((max(len(kinds), 1), depth, width), jnp.bfloat16),
            pltpu.SemaphoreType.DMA((8,)),
            pltpu.SemaphoreType.DMA((max(len(kinds), 1),)),
        ],
        compiler_params=PARAMS,
        cost_estimate=pl.CostEstimate(
            flops=6 * queries.size * HD, bytes_accessed=10 << 20, transcendentals=queries.size
        ),
        name="attend",
    )(*arrays, features)


def chunk_kernel(jobs, features, half_a, half_b, *refs):
    kinds = [kind for kind, _ in jobs]
    count = sum(len(which) for _, which in jobs)
    outs, (blocks, sems) = refs[:count], refs[count:]
    copies = start_features(features, kinds, blocks, sems)
    cots = (half_a, half_b)
    place = 0
    for i, (_, which) in enumerate(jobs):
        copies[i].wait()
        for h in which:
            outs[place][...] = jnp.dot(
                cots[h][...], blocks[i], preferred_element_type=jnp.float32
            )
            place += 1


def chunks(jobs, features, halves, width):
    depth = features.shape[0]
    half = halves[0].shape[0]
    count = sum(len(which) for _, which in jobs)
    vmem = pl.BlockSpec(memory_space=pltpu.VMEM)
    return pl.pallas_call(
        functools.partial(chunk_kernel, jobs),
        in_specs=[HBM, vmem, vmem],
        out_specs=[vmem] * count,
        out_shape=[jax.ShapeDtypeStruct((half, width), jnp.float32)] * count,
        scratch_shapes=[
            pltpu.VMEM((len(jobs), depth, width), jnp.bfloat16),
            pltpu.SemaphoreType.DMA((len(jobs),)),
        ],
        compiler_params=PARAMS,
        cost_estimate=pl.CostEstimate(
            flops=2 * depth * width * half * count,
            bytes_accessed=2 * depth * width * len(jobs) + 4 * half * width * count,
            transcendentals=0,
        ),
        name="chunk",
    )(features, *halves)


def finish_kernel(half, count, *refs):
    grad, peaks = refs[-2:]
    total = refs[0][...]
    for ref in refs[1:count]:
        total = total + ref[...]
    buckets = total.shape[0] // BUCKET
    lane = lax.broadcasted_iota(jnp.int32, peaks.shape, 1)
    peak = refs[count + 1][...] if len(refs) > count + 2 else jnp.zeros(peaks.shape, jnp.float32)
    for b in range(buckets):
        top = jnp.abs(total[b * BUCKET : (b + 1) * BUCKET])
        top = jnp.max(jnp.max(top, axis=0, keepdims=True), axis=1, keepdims=True)
        peak = jnp.where(lane == half * buckets + b, top, peak)
    peaks[...] = peak
    grad[...] = total.T


def finish(half, parts, grad, peaks, columns):
    size, width = parts[0].shape
    count = len(parts)
    whole = pl.BlockSpec((size, width), lambda i: (0, 0))
    tile = pl.BlockSpec((8, 128), lambda i: (0, 0))
    in_specs = [whole] * count
    args = list(parts)
    aliases = {}
    if grad is not None:
        in_specs += [pl.BlockSpec(memory_space=pl.ANY), tile]
        args += [grad, peaks]
        aliases = {count: 0}
    return pl.pallas_call(
        functools.partial(finish_kernel, half, count),
        grid=(1,),
        in_specs=in_specs,
        out_specs=[pl.BlockSpec((width, size), lambda i: (0, half)), tile],
        out_shape=[
            jax.ShapeDtypeStruct((width, columns), jnp.float32),
            jax.ShapeDtypeStruct((8, 128), jnp.float32),
        ],
        input_output_aliases=aliases,
        compiler_params=PARAMS,
        name="finish",
    )(*args)


def reduce_on_grid(features, halves, firsts, dp):
    width = features.shape[1] // dp
    columns = 2 * halves[0].shape[0]
    rank = lax.axis_index("dp")
    edge = (rank < 2) | (rank >= 6)

    def across(x):
        return lax.ppermute(x, "dp", [(r, r ^ 1) for r in range(dp)])

    def pair(x):
        return lax.ppermute(x, "dp", [(r, r ^ 2) for r in range(dp)])

    def outward(x):
        return lax.ppermute(x, "dp", [(r, r ^ 2) for r in (0, 1, 6, 7)])

    def middle(x):
        return lax.ppermute(x, "dp", [(r, r ^ 6) for r in (2, 3, 4, 5)])

    def make(*jobs):
        return chunks(jobs, features, halves, width)

    a, b = 0, 1
    cross3a, crosspa = firsts
    cross3b, ownpa = make(((FAR3, CROSS), (b,)), ((PAIR, SAME), (a,)))
    cross2a, cross2b, own3a, own3b = make(((FAR2, CROSS), (a, b)), ((FAR3, SAME), (a, b)))
    crosspb, own2a, own2b = make(((PAIR, CROSS), (b,)), ((FAR2, SAME), (a, b)))
    crossoa, crossob, ownpb = make(((OWN, CROSS), (a, b)), ((PAIR, SAME), (b,)))
    ownoa, ownob = make(((OWN, SAME), (a, b)))

    y0 = across(cross3a)
    e0 = pair(crosspa)
    y1 = across(cross3b)
    e1 = outward(ownpa)
    y2 = across(cross2a)
    e2 = outward(own3a + y0)
    y3 = across(cross2b)
    e3 = outward(own3b + y1)
    m3 = middle(own3a + y0 + e2)
    y4 = across(crosspb)
    e4 = outward(own2a + y2)
    m4 = middle(own3b + y1 + e3)
    y5 = across(crossoa + e0)
    cut = own2b.shape[0] // 2
    e5 = []
    for part in (slice(0, cut), slice(cut, None)):
        e5.append(
            pair(jnp.where(edge, own2b[part] + y3[part], ownpa[part] + m3[part]))
        )
    m5 = middle(own2a + y2 + e4)
    y6 = across(crossob)
    e6 = pair(ownpb + y4 + m4)
    m6 = []
    for i, part in enumerate((slice(0, cut), slice(cut, None))):
        m6.append(middle(own2b[part] + y3[part] + e5[i]))
    arrived = jnp.where(edge, jnp.concatenate(e5, axis=0), e1)
    grad, peaks = finish(a, [ownoa, y5, arrived, m5], None, None, columns)
    grad, peaks = finish(b, [ownob, y6, e6, jnp.concatenate(m6, axis=0)], grad, peaks, columns)
    for hop in (1, 2, 4):
        peaks = jnp.maximum(
            peaks, lax.ppermute(peaks, "dp", [(r, r ^ hop) for r in range(dp)])
        )
    return grad, peaks[0, : columns // BUCKET]


def reduce_plain(features, halves):
    cots = jnp.concatenate(halves, axis=0)
    partial_grad = lax.dot_general(
        features, cots, (((0,), (1,)), ((), ())), preferred_element_type=jnp.float32
    )
    grad = lax.psum_scatter(partial_grad, "dp", scatter_dimension=0, tiled=True)
    peaks = jnp.max(jnp.abs(grad).reshape(-1, cots.shape[0] // BUCKET, BUCKET), axis=(0, 2))
    return grad, lax.pmax(peaks, "dp")


def per_device(
    dp,
    queries,
    cache_keys,
    cache_values,
    new_keys,
    new_values,
    features,
    cotangent,
    rewards,
    lengths,
):
    flat = features.reshape(-1, features.shape[2])
    arrays = (
        lengths,
        rewards,
        queries,
        cache_keys,
        cache_values,
        new_keys,
        new_values,
        cotangent,
    )
    on_grid = dp == 8
    kinds = ((FAR3, CROSS), (PAIR, CROSS)) if on_grid else ()
    width = features.shape[2] // 8 if on_grid else BUCKET
    attended, half_a, half_b, *firsts = begin(arrays, flat, kinds, width)
    if on_grid:
        grad, peaks = reduce_on_grid(flat, (half_a, half_b), firsts, dp)
    else:
        grad, peaks = reduce_plain(flat, (half_a, half_b))
    return attended, grad, peaks


def solution(mesh):
    split = P(("groups", "dp"), None, "tensor")
    rows = P(("groups", "dp"))
    in_specs = (
        split,
        split,
        split,
        split,
        split,
        P(("groups", "dp"), None, None),
        split,
        rows,
        rows,
    )
    out_specs = (split, P(("groups", "dp"), "tensor"), P(("groups", "tensor")))
    return jax.shard_map(
        functools.partial(per_device, mesh.shape["dp"]),
        mesh=mesh,
        in_specs=in_specs,
        out_specs=out_specs,
        check_vma=False,
    )
```

```python
import functools
import math

import jax
import jax.numpy as jnp
from jax import lax
from jax.experimental import pallas as pl
from jax.experimental.pallas import tpu as pltpu
from jax.sharding import PartitionSpec as P

HD = 128
GROUP = 8
BUCKET = 128
BATCH = 16
VMEM_BYTES = 20 * 1024 * 1024
HBM = pl.BlockSpec(memory_space=pltpu.HBM)
PARAMS = pltpu.CompilerParams(vmem_limit_bytes=VMEM_BYTES)
MIDDLE = pltpu.CompilerParams(vmem_limit_bytes=46 * 1024 * 1024)
WIDE = pltpu.CompilerParams(vmem_limit_bytes=60 * 1024 * 1024)
SMALL = pl.CostEstimate(flops=1000, bytes_accessed=1000, transcendentals=0)
FAR3, FAR2, PAIR, OWN = range(4)
CROSS, SAME = True, False


def advantage_rows(rewards):
    advantages = []
    for base in range(0, rewards.shape[0], GROUP):
        centre = rewards[base]
        for i in range(1, GROUP):
            centre = centre + rewards[base + i]
        centre = centre * (1.0 / GROUP)
        spread = (rewards[base] - centre) * (rewards[base] - centre)
        for i in range(1, GROUP):
            spread = spread + (rewards[base + i] - centre) * (rewards[base + i] - centre)
        spread = jnp.sqrt(jnp.full((1, HD), spread * (1.0 / GROUP), jnp.float32))
        spread = jnp.maximum(spread, 1.0)
        for r in range(base, base + GROUP):
            advantages.append(jnp.full((1, HD), rewards[r] - centre, jnp.float32) / spread)
    return advantages


def attend_heads(lengths, rewards, q, ck, nk, cv=None, nv=None, out=None, cot=None, rows=None):
    rollouts, steps, width = q.shape
    key_heads = ck.shape[2] // HD
    heads = width // HD // key_heads
    ctx = ck.shape[1]
    slots = ctx + steps
    padded = -(-slots // HD) * HD
    pad = padded - slots
    scaling = 1.0 / math.sqrt(HD)

    def by_head(ref, r, g):
        return jnp.concatenate(
            [
                ref[r, :, (g * heads + j) * HD : (g * heads + j + 1) * HD].astype(jnp.float32)
                for j in range(heads)
            ],
            axis=0,
        )

    def joined(past, fresh, r, g):
        lanes = slice(g * HD, (g + 1) * HD)
        fresh = jnp.concatenate(
            [fresh[r, :, lanes].astype(jnp.float32), jnp.zeros((pad, HD), jnp.float32)], axis=0
        ).astype(jnp.bfloat16)
        return jnp.concatenate([past[r, :, lanes], fresh], axis=0)

    shape = (heads * steps, padded)
    column = lax.broadcasted_iota(jnp.int32, shape, 1)
    step = lax.broadcasted_iota(jnp.int32, shape, 0) % steps
    fresh_live = (column >= ctx) & (column - ctx <= step)
    advantages = advantage_rows(rewards) if rows is not None else None
    lives = []
    for r in range(rollouts):
        lives.append((column < lengths[r]) | fresh_live)
    units = [(r, g) for g in range(key_heads) for r in range(rollouts)]
    for start in range(0, len(units), BATCH):
        batch = units[start : start + BATCH]
        scores = [
            lax.dot_general(
                by_head(q, r, g).astype(jnp.bfloat16),
                joined(ck, nk, r, g),
                (((1,), (1,)), ((), ())),
                preferred_element_type=jnp.float32,
            )
            for r, g in batch
        ]
        scores = [
            jnp.where(lives[r], x * scaling, -1e30) for (r, g), x in zip(batch, scores)
        ]
        highest = [jnp.max(x, axis=1, keepdims=True) for x in scores]
        lift = [jnp.exp(x - top) for x, top in zip(scores, highest)]
        totals = [jnp.sum(x, axis=1, keepdims=True) for x in lift]
        weights = [(x / total).astype(jnp.bfloat16) for x, total in zip(lift, totals)]
        if out is not None:
            results = [
                jnp.dot(w, joined(cv, nv, r, g), preferred_element_type=jnp.float32)
                for (r, g), w in zip(batch, weights)
            ]
            for (r, g), result in zip(batch, results):
                for j in range(heads):
                    out[r, :, (g * heads + j) * HD : (g * heads + j + 1) * HD] = result[
                        j * steps : (j + 1) * steps
                    ].astype(jnp.bfloat16)
        if rows is not None:
            value_cots = [
                lax.dot_general(
                    w,
                    (by_head(cot, r, g) * advantages[r]).astype(jnp.bfloat16),
                    (((0,), (0,)), ((), ())),
                    preferred_element_type=jnp.float32,
                )
                for (r, g), w in zip(batch, weights)
            ]
            for (r, g), value_cot in zip(batch, value_cots):
                rows[r * slots : (r + 1) * slots, g * HD : (g + 1) * HD] = value_cot[:slots]


def block_of(kind):
    plane_kind, cross = kind
    rank = lax.axis_index("dp")
    plane = rank // 2
    row = rank - plane * 2
    low = plane < 2
    if plane_kind == FAR3:
        target = jnp.where(low, 3, 0)
    elif plane_kind == FAR2:
        target = jnp.where(low, 2, 1)
    elif plane_kind == PAIR:
        target = plane + 1 - 2 * (plane - (plane // 2) * 2)
    else:
        target = plane
    return target * 2 + (1 - row if cross else row)


def start_features(features, kinds, buffers, sems):
    copies = []
    for i, kind in enumerate(kinds):
        width = buffers.shape[2]
        first = pl.multiple_of(block_of(kind) * width, HD)
        copy = pltpu.make_async_copy(
            features.at[:, pl.ds(first, width)], buffers.at[i], sems.at[i]
        )
        copy.start()
        copies.append(copy)
    return copies


def copy_all(sources, buffers, sems):
    copies = []
    for i, (source, buffer) in enumerate(zip(sources, buffers)):
        copy = pltpu.make_async_copy(source, buffer, sems.at[i])
        copy.start()
        copies.append(copy)
    return copies


def lanes_of(ref, half):
    size = ref.shape[-1] // 2
    return ref.at[:, :, pl.ds(half * size, size)]


def begin_kernel(half, jobs, *refs):
    ins, refs = refs[:6], refs[6:]
    features, refs = refs[0], refs[1:]
    cots = []
    if half:
        cots.append(refs[0])
        refs = refs[1:]
    cot_half, refs = refs[0], refs[1:]
    outs, refs = refs[: len(jobs)], refs[len(jobs) :]
    bufs, (rows, blocks, sems, block_sems) = refs[:6], refs[6:]
    sources = list(ins[:2]) + [lanes_of(ref, half) for ref in ins[2:]]
    copies = copy_all(sources, bufs, sems)
    kinds = [kind for kind, _ in jobs]
    block_copies = start_features(features, kinds, blocks, block_sems)
    for copy in copies:
        copy.wait()
    lengths, rewards, q, ck, nk, cot = bufs
    attend_heads(lengths, rewards, q, ck, nk, cot=cot, rows=rows)
    cot_half[...] = rows[...].T.astype(jnp.bfloat16)
    cots.append(cot_half)
    for i, (_, h) in enumerate(jobs):
        block_copies[i].wait()
        outs[i][...] = jnp.dot(cots[h][...], blocks[i], preferred_element_type=jnp.float32)


def begin(half, jobs, arrays, features, cots, width):
    lengths, rewards, queries, ck, _, _ = arrays
    depth = features.shape[0]
    columns = ck.shape[2] // 2
    shapes = [jax.ShapeDtypeStruct((columns, depth), jnp.bfloat16)]
    shapes += [jax.ShapeDtypeStruct((columns, width), jnp.float32)] * len(jobs)
    vmem = pl.BlockSpec(memory_space=pltpu.VMEM)
    return pl.pallas_call(
        functools.partial(begin_kernel, half, jobs),
        in_specs=[HBM] * 7 + [vmem] * len(cots),
        out_specs=[vmem] * len(shapes),
        out_shape=shapes,
        scratch_shapes=[pltpu.SMEM(x.shape, x.dtype) for x in arrays[:2]]
        + [pltpu.VMEM(x.shape[:2] + (x.shape[2] // 2,), x.dtype) for x in arrays[2:]]
        + [
            pltpu.VMEM((depth, columns), jnp.float32),
            pltpu.VMEM((max(len(jobs), 1), depth, width), jnp.bfloat16),
            pltpu.SemaphoreType.DMA((6,)),
            pltpu.SemaphoreType.DMA((max(len(jobs), 1),)),
        ],
        compiler_params=WIDE,
        cost_estimate=SMALL,
        name="value_cot",
    )(*arrays, features, *cots)


def attended_kernel(*refs):
    ins, out, bufs, sems = refs[:6], refs[6], refs[7:13], refs[13]
    for copy in copy_all(ins, bufs, sems):
        copy.wait()
    lengths, queries, ck, nk, cv, nv = bufs
    attend_heads(lengths, None, queries, ck, nk, cv=cv, nv=nv, out=out)


def attend(*arrays):
    queries = arrays[1]
    return pl.pallas_call(
        attended_kernel,
        in_specs=[HBM] * 6,
        out_specs=pl.BlockSpec(memory_space=pltpu.VMEM),
        out_shape=jax.ShapeDtypeStruct(queries.shape, jnp.bfloat16),
        scratch_shapes=[pltpu.SMEM(arrays[0].shape, arrays[0].dtype)]
        + [pltpu.VMEM(x.shape, x.dtype) for x in arrays[1:]]
        + [pltpu.SemaphoreType.DMA((6,))],
        compiler_params=MIDDLE,
        cost_estimate=SMALL,
        name="attend",
    )(*arrays)


def chunk_kernel(jobs, features, half_a, half_b, *refs):
    kinds = [kind for kind, _ in jobs]
    count = sum(len(which) for _, which in jobs)
    outs, (blocks, sems) = refs[:count], refs[count:]
    copies = start_features(features, kinds, blocks, sems)
    cots = (half_a, half_b)
    place = 0
    for i, (_, which) in enumerate(jobs):
        copies[i].wait()
        for h in which:
            outs[place][...] = jnp.dot(
                cots[h][...], blocks[i], preferred_element_type=jnp.float32
            )
            place += 1


def chunks(jobs, features, halves, width):
    depth = features.shape[0]
    half = halves[0].shape[0]
    count = sum(len(which) for _, which in jobs)
    vmem = pl.BlockSpec(memory_space=pltpu.VMEM)
    return pl.pallas_call(
        functools.partial(chunk_kernel, jobs),
        in_specs=[HBM, vmem, vmem],
        out_specs=[vmem] * count,
        out_shape=[jax.ShapeDtypeStruct((half, width), jnp.float32)] * count,
        scratch_shapes=[
            pltpu.VMEM((len(jobs), depth, width), jnp.bfloat16),
            pltpu.SemaphoreType.DMA((len(jobs),)),
        ],
        compiler_params=MIDDLE,
        cost_estimate=SMALL,
        name="chunk",
    )(features, *halves)


def add_kernel(half, edge_first, *refs):
    count = len(refs) - 3
    total, peaks = refs[-2:]
    size = total.shape[0]
    cut = size // 2
    for b in range(2):
        rows = slice(b * cut, (b + 1) * cut)
        part = None
        for ref in refs[:2]:
            part = ref[rows] if part is None else part + ref[rows]
        if edge_first:
            rank = lax.axis_index("dp")
            edge = (rank < 2) | (rank >= 6)
            part = part + jnp.where(edge, refs[2 + b][...], refs[4][rows])
            part = part + refs[5][rows]
        else:
            part = part + refs[2][rows] + refs[3 + b][...]
        total[rows] = part
    buckets = size // BUCKET
    lane = lax.broadcasted_iota(jnp.int32, peaks.shape, 1)
    peak = refs[count][...]
    for b in range(buckets):
        top = jnp.abs(total[b * BUCKET : (b + 1) * BUCKET])
        top = jnp.max(jnp.max(top, axis=0, keepdims=True), axis=1, keepdims=True)
        peak = jnp.where(lane == half * buckets + b, top, peak)
    peaks[...] = peak


def add_parts(half, edge_first, parts, peaks):
    vmem = pl.BlockSpec(memory_space=pltpu.VMEM)
    return pl.pallas_call(
        functools.partial(add_kernel, half, edge_first),
        in_specs=[vmem] * (len(parts) + 1),
        out_specs=[vmem] * 2,
        out_shape=[
            jax.ShapeDtypeStruct(parts[0].shape, jnp.float32),
            jax.ShapeDtypeStruct(peaks.shape, jnp.float32),
        ],
        compiler_params=PARAMS,
        cost_estimate=SMALL,
        name="add_parts",
    )(*parts, peaks)


def place_kernel(total, *refs):
    refs[-1][...] = total[...].T


def place(half, total, grad, columns):
    size, width = total.shape
    in_specs = [pl.BlockSpec(memory_space=pltpu.VMEM)]
    args = [total]
    aliases = {}
    if grad is not None:
        in_specs.append(pl.BlockSpec(memory_space=pl.ANY))
        args.append(grad)
        aliases = {1: 0}
    return pl.pallas_call(
        place_kernel,
        grid=(1,),
        in_specs=in_specs,
        out_specs=pl.BlockSpec((width, size), lambda i: (0, half)),
        out_shape=jax.ShapeDtypeStruct((width, columns), jnp.float32),
        input_output_aliases=aliases,
        compiler_params=PARAMS,
        cost_estimate=SMALL,
        name="place",
    )(*args)


def reduce_on_grid(features, halves, firsts, attended, dp):
    width = features.shape[1] // dp
    columns = 2 * halves[0].shape[0]
    rank = lax.axis_index("dp")
    edge = (rank < 2) | (rank >= 6)

    def across(x):
        return lax.ppermute(x, "dp", [(r, r ^ 1) for r in range(dp)])

    def pair(x):
        return lax.ppermute(x, "dp", [(r, r ^ 2) for r in range(dp)])

    def outward(x):
        return lax.ppermute(x, "dp", [(r, r ^ 2) for r in (0, 1, 6, 7)])

    def middle(x):
        return lax.ppermute(x, "dp", [(r, r ^ 6) for r in (2, 3, 4, 5)])

    def together(*arrays):
        return lax.optimization_barrier(arrays)

    def make(*jobs):
        return chunks(jobs, features, halves, width)

    a, b = 0, 1
    cross3a, crosspa, cross3b, ownpa = firsts
    (own3a, own3b, cross2a, cross2b, own2a, own2b, crosspb, crossoa, crossob, ownpb, ownoa, ownob) = (
        make(
            ((FAR3, SAME), (a, b)),
            ((FAR2, CROSS), (a, b)),
            ((FAR2, SAME), (a, b)),
            ((PAIR, CROSS), (b,)),
            ((OWN, CROSS), (a, b)),
            ((PAIR, SAME), (b,)),
            ((OWN, SAME), (a, b)),
        )
    )

    y0, e0 = together(across(cross3a), pair(crosspa))
    y1, e1 = together(across(cross3b), outward(ownpa))
    y2, e2, attended = together(across(cross2a), outward(own3a + y0), attended)
    y3, e3 = together(across(cross2b), outward(own3b + y1))
    m3 = middle(own3a + y0 + e2)
    y4, e4 = together(across(crosspb), outward(own2a + y2))
    m4 = middle(own3b + y1 + e3)
    y5 = across(crossoa + e0)
    cut = own2b.shape[0] // 2
    e5 = []
    for part in (slice(0, cut), slice(cut, None)):
        e5.append(
            pair(jnp.where(edge, own2b[part] + y3[part], ownpa[part] + m3[part]))
        )
    m5 = middle(own2a + y2 + e4)
    y6 = across(crossob)
    e6 = pair(ownpb + y4 + m4)
    m6 = []
    for i, part in enumerate((slice(0, cut), slice(cut, None))):
        (send,) = together(own2b[part] + y3[part] + e5[i])
        m6.append(middle(send))
    peaks = jnp.zeros((8, HD), jnp.float32)
    total, peaks = add_parts(a, True, [ownoa, y5, *e5, e1, m5], peaks)
    grad, peaks = together(place(a, total, None, columns), peaks)
    total, peaks = add_parts(b, False, [ownob, y6, e6, *m6], peaks)
    grad = place(b, total, grad, columns)
    for hop in (1, 2, 4):
        peaks = jnp.maximum(
            peaks, lax.ppermute(peaks, "dp", [(r, r ^ hop) for r in range(dp)])
        )
    return attended, grad, peaks[0, : columns // BUCKET]


def reduce_plain(features, halves):
    cots = jnp.concatenate(halves, axis=0)
    partial_grad = lax.dot_general(
        features, cots, (((0,), (1,)), ((), ())), preferred_element_type=jnp.float32
    )
    grad = lax.psum_scatter(partial_grad, "dp", scatter_dimension=0, tiled=True)
    peaks = jnp.max(jnp.abs(grad).reshape(-1, cots.shape[0] // BUCKET, BUCKET), axis=(0, 2))
    return grad, lax.pmax(peaks, "dp")


def per_device(
    dp,
    queries,
    cache_keys,
    cache_values,
    new_keys,
    new_values,
    features,
    cotangent,
    rewards,
    lengths,
):
    flat = features.reshape(-1, features.shape[2])
    arrays = (lengths, rewards, queries, cache_keys, new_keys, cotangent)
    on_grid = dp == 8
    width = features.shape[2] // 8 if on_grid else BUCKET
    jobs_a = (((FAR3, CROSS), 0), ((PAIR, CROSS), 0)) if on_grid else ()
    jobs_b = (((FAR3, CROSS), 1), ((PAIR, SAME), 0)) if on_grid else ()
    half_a, *firsts = begin(0, jobs_a, arrays, flat, [], width)
    half_b, *seconds = begin(1, jobs_b, arrays, flat, [half_a], width)
    attended = attend(lengths, queries, cache_keys, new_keys, cache_values, new_values)
    firsts += seconds
    if on_grid:
        attended, grad, peaks = reduce_on_grid(
            flat, (half_a, half_b), firsts, attended, dp
        )
    else:
        grad, peaks = reduce_plain(flat, (half_a, half_b))
    return attended, grad, peaks


def solution(mesh):
    split = P(("groups", "dp"), None, "tensor")
    rows = P(("groups", "dp"))
    in_specs = (
        split,
        split,
        split,
        split,
        split,
        P(("groups", "dp"), None, None),
        split,
        rows,
        rows,
    )
    out_specs = (split, P(("groups", "dp"), "tensor"), P(("groups", "tensor")))
    return jax.shard_map(
        functools.partial(per_device, mesh.shape["dp"]),
        mesh=mesh,
        in_specs=in_specs,
        out_specs=out_specs,
        check_vma=False,
    )
```

```python
import functools
import math

import jax
import jax.numpy as jnp
from jax import lax
from jax.experimental import pallas as pl
from jax.experimental.pallas import tpu as pltpu
from jax.sharding import PartitionSpec as P

HD = 128
GROUP = 8
BUCKET = 128
BATCH = 16
EARLY = 2
VMEM_BYTES = 20 * 1024 * 1024
HBM = pl.BlockSpec(memory_space=pltpu.HBM)
PARAMS = pltpu.CompilerParams(vmem_limit_bytes=VMEM_BYTES)
MIDDLE = pltpu.CompilerParams(vmem_limit_bytes=46 * 1024 * 1024)
WIDE = pltpu.CompilerParams(vmem_limit_bytes=60 * 1024 * 1024)
SMALL = pl.CostEstimate(flops=1000, bytes_accessed=1000, transcendentals=0)
FAR3, FAR2, PAIR, OWN = range(4)
CROSS, SAME = True, False


def advantage_rows(rewards):
    advantages = []
    for base in range(0, rewards.shape[0], GROUP):
        centre = rewards[base]
        for i in range(1, GROUP):
            centre = centre + rewards[base + i]
        centre = centre * (1.0 / GROUP)
        spread = (rewards[base] - centre) * (rewards[base] - centre)
        for i in range(1, GROUP):
            spread = spread + (rewards[base + i] - centre) * (rewards[base + i] - centre)
        spread = jnp.sqrt(jnp.full((1, HD), spread * (1.0 / GROUP), jnp.float32))
        spread = jnp.maximum(spread, 1.0)
        for r in range(base, base + GROUP):
            advantages.append(jnp.full((1, HD), rewards[r] - centre, jnp.float32) / spread)
    return advantages


def attend_heads(lengths, rewards, q, ck, nk, cv=None, nv=None, out=None, cot=None, rows=None):
    rollouts, steps, width = q.shape
    key_heads = ck.shape[2] // HD
    heads = width // HD // key_heads
    ctx = ck.shape[1]
    slots = ctx + steps
    padded = -(-slots // HD) * HD
    pad = padded - slots
    scaling = 1.0 / math.sqrt(HD)

    def by_head(ref, r, g):
        return jnp.concatenate(
            [
                ref[r, :, (g * heads + j) * HD : (g * heads + j + 1) * HD].astype(jnp.float32)
                for j in range(heads)
            ],
            axis=0,
        )

    def joined(past, fresh, r, g):
        lanes = slice(g * HD, (g + 1) * HD)
        fresh = jnp.concatenate(
            [fresh[r, :, lanes].astype(jnp.float32), jnp.zeros((pad, HD), jnp.float32)], axis=0
        ).astype(jnp.bfloat16)
        return jnp.concatenate([past[r, :, lanes], fresh], axis=0)

    shape = (heads * steps, padded)
    column = lax.broadcasted_iota(jnp.int32, shape, 1)
    step = lax.broadcasted_iota(jnp.int32, shape, 0) % steps
    fresh_live = (column >= ctx) & (column - ctx <= step)
    advantages = advantage_rows(rewards) if rows is not None else None
    lives = []
    for r in range(rollouts):
        lives.append((column < lengths[r]) | fresh_live)
    units = [(r, g) for g in range(key_heads) for r in range(rollouts)]
    for start in range(0, len(units), BATCH):
        batch = units[start : start + BATCH]
        scores = [
            lax.dot_general(
                by_head(q, r, g).astype(jnp.bfloat16),
                joined(ck, nk, r, g),
                (((1,), (1,)), ((), ())),
                preferred_element_type=jnp.float32,
            )
            for r, g in batch
        ]
        scores = [
            jnp.where(lives[r], x * scaling, -1e30) for (r, g), x in zip(batch, scores)
        ]
        highest = [jnp.max(x, axis=1, keepdims=True) for x in scores]
        lift = [jnp.exp(x - top) for x, top in zip(scores, highest)]
        totals = [jnp.sum(x, axis=1, keepdims=True) for x in lift]
        weights = [(x / total).astype(jnp.bfloat16) for x, total in zip(lift, totals)]
        if out is not None:
            results = [
                jnp.dot(w, joined(cv, nv, r, g), preferred_element_type=jnp.float32)
                for (r, g), w in zip(batch, weights)
            ]
            for (r, g), result in zip(batch, results):
                for j in range(heads):
                    out[r, :, (g * heads + j) * HD : (g * heads + j + 1) * HD] = result[
                        j * steps : (j + 1) * steps
                    ].astype(jnp.bfloat16)
        if rows is not None:
            value_cots = [
                lax.dot_general(
                    w,
                    (by_head(cot, r, g) * advantages[r]).astype(jnp.bfloat16),
                    (((0,), (0,)), ((), ())),
                    preferred_element_type=jnp.float32,
                )
                for (r, g), w in zip(batch, weights)
            ]
            for (r, g), value_cot in zip(batch, value_cots):
                rows[r * slots : (r + 1) * slots, g * HD : (g + 1) * HD] = value_cot[:slots]


def block_of(kind):
    plane_kind, cross = kind
    rank = lax.axis_index("dp")
    plane = rank // 2
    row = rank - plane * 2
    low = plane < 2
    if plane_kind == FAR3:
        target = jnp.where(low, 3, 0)
    elif plane_kind == FAR2:
        target = jnp.where(low, 2, 1)
    elif plane_kind == PAIR:
        target = plane + 1 - 2 * (plane - (plane // 2) * 2)
    else:
        target = plane
    return target * 2 + (1 - row if cross else row)


def start_features(features, kinds, buffers, sems):
    copies = []
    for i, kind in enumerate(kinds):
        width = buffers.shape[2]
        first = pl.multiple_of(block_of(kind) * width, HD)
        copy = pltpu.make_async_copy(
            features.at[:, pl.ds(first, width)], buffers.at[i], sems.at[i]
        )
        copy.start()
        copies.append(copy)
    return copies


def copy_all(sources, buffers, sems):
    copies = []
    for i, (source, buffer) in enumerate(zip(sources, buffers)):
        copy = pltpu.make_async_copy(source, buffer, sems.at[i])
        copy.start()
        copies.append(copy)
    return copies


def lanes_of(ref, half):
    size = ref.shape[-1] // 2
    return ref.at[:, :, pl.ds(half * size, size)]


def begin_kernel(half, jobs, *refs):
    ins, refs = refs[:6], refs[6:]
    features, refs = refs[0], refs[1:]
    cot_half, refs = refs[0], refs[1:]
    outs, refs = refs[: len(jobs)], refs[len(jobs) :]
    bufs, (rows, blocks, sems, block_sems) = refs[:6], refs[6:]
    sources = list(ins[:2]) + [lanes_of(ref, half) for ref in ins[2:]]
    copies = copy_all(sources, bufs, sems)
    kinds = [kind for job in jobs for kind, _ in job]
    block_copies = start_features(features, kinds, blocks, block_sems)
    for copy in copies:
        copy.wait()
    lengths, rewards, q, ck, nk, cot = bufs
    attend_heads(lengths, rewards, q, ck, nk, cot=cot, rows=rows)
    cots = rows[...].T.astype(jnp.bfloat16)
    cot_half[...] = cots
    place = 0
    for out, job in zip(outs, jobs):
        first = 0
        for _, size in job:
            block_copies[place].wait()
            out[first : first + size] = jnp.dot(
                cots[:size], blocks[place], preferred_element_type=jnp.float32
            )
            first += size
            place += 1


def begin(half, jobs, arrays, features, width):
    lengths, rewards, queries, ck, _, _ = arrays
    depth = features.shape[0]
    columns = ck.shape[2] // 2
    count = max(sum(len(job) for job in jobs), 1)
    shapes = [jax.ShapeDtypeStruct((columns, depth), jnp.bfloat16)]
    for job in jobs:
        shapes.append(jax.ShapeDtypeStruct((sum(size for _, size in job), width), jnp.float32))
    vmem = pl.BlockSpec(memory_space=pltpu.VMEM)
    return pl.pallas_call(
        functools.partial(begin_kernel, half, jobs),
        in_specs=[HBM] * 7,
        out_specs=[vmem] * len(shapes),
        out_shape=shapes,
        scratch_shapes=[pltpu.SMEM(x.shape, x.dtype) for x in arrays[:2]]
        + [pltpu.VMEM(x.shape[:2] + (x.shape[2] // 2,), x.dtype) for x in arrays[2:]]
        + [
            pltpu.VMEM((depth, columns), jnp.float32),
            pltpu.VMEM((count, depth, width), jnp.bfloat16),
            pltpu.SemaphoreType.DMA((6,)),
            pltpu.SemaphoreType.DMA((count,)),
        ],
        compiler_params=WIDE,
        cost_estimate=SMALL,
        name="value_cot",
    )(*arrays, features)


def attended_kernel(*refs):
    ins, out, bufs, sems = refs[:6], refs[6], refs[7:13], refs[13]
    for copy in copy_all(ins, bufs, sems):
        copy.wait()
    lengths, queries, ck, nk, cv, nv = bufs
    attend_heads(lengths, None, queries, ck, nk, cv=cv, nv=nv, out=out)


def attend(*arrays):
    queries = arrays[1]
    return pl.pallas_call(
        attended_kernel,
        in_specs=[HBM] * 6,
        out_specs=pl.BlockSpec(memory_space=pltpu.VMEM),
        out_shape=jax.ShapeDtypeStruct(queries.shape, jnp.bfloat16),
        scratch_shapes=[pltpu.SMEM(arrays[0].shape, arrays[0].dtype)]
        + [pltpu.VMEM(x.shape, x.dtype) for x in arrays[1:]]
        + [pltpu.SemaphoreType.DMA((6,))],
        compiler_params=MIDDLE,
        cost_estimate=SMALL,
        name="attend",
    )(*arrays)


def chunk_kernel(jobs, features, half_a, half_b, *refs):
    kinds = [kind for kind, _ in jobs]
    count = sum(len(which) for _, which in jobs)
    outs, (blocks, sems) = refs[:count], refs[count:]
    copies = start_features(features, kinds, blocks, sems)
    cots = (half_a, half_b)
    place = 0
    for i, (_, which) in enumerate(jobs):
        copies[i].wait()
        for h in which:
            outs[place][...] = jnp.dot(
                cots[h][...], blocks[i], preferred_element_type=jnp.float32
            )
            place += 1


def chunks(jobs, features, halves, width):
    depth = features.shape[0]
    half = halves[0].shape[0]
    count = sum(len(which) for _, which in jobs)
    vmem = pl.BlockSpec(memory_space=pltpu.VMEM)
    return pl.pallas_call(
        functools.partial(chunk_kernel, jobs),
        in_specs=[HBM, vmem, vmem],
        out_specs=[vmem] * count,
        out_shape=[jax.ShapeDtypeStruct((half, width), jnp.float32)] * count,
        scratch_shapes=[
            pltpu.VMEM((len(jobs), depth, width), jnp.bfloat16),
            pltpu.SemaphoreType.DMA((len(jobs),)),
        ],
        compiler_params=MIDDLE,
        cost_estimate=SMALL,
        name="chunk",
    )(features, *halves)


def add_kernel(half, cut, *refs):
    count = len(refs) - 3
    total, peaks = refs[-2:]
    size = total.shape[0]
    last = refs[count - 1][...]
    if not half:
        piece = jnp.concatenate([refs[3][size:], refs[4][...]], axis=0)
        rank = lax.axis_index("dp")
        last = jnp.where((rank < 2) | (rank >= 6), last, piece)
    total[...] = refs[0][...] + refs[1][half * size : (half + 1) * size] + refs[2][...] + last
    buckets = size // BUCKET
    lane = lax.broadcasted_iota(jnp.int32, peaks.shape, 1)
    peak = refs[count][...]
    for b in range(buckets):
        top = jnp.abs(total[b * BUCKET : (b + 1) * BUCKET])
        top = jnp.max(jnp.max(top, axis=0, keepdims=True), axis=1, keepdims=True)
        peak = jnp.where(lane == half * buckets + b, top, peak)
    peaks[...] = peak


def add_parts(half, cut, parts, peaks):
    vmem = pl.BlockSpec(memory_space=pltpu.VMEM)
    return pl.pallas_call(
        functools.partial(add_kernel, half, cut),
        in_specs=[vmem] * (len(parts) + 1),
        out_specs=[vmem] * 2,
        out_shape=[
            jax.ShapeDtypeStruct(parts[0].shape, jnp.float32),
            jax.ShapeDtypeStruct(peaks.shape, jnp.float32),
        ],
        compiler_params=PARAMS,
        cost_estimate=SMALL,
        name="add_parts",
    )(*parts, peaks)


def place_kernel(total, *refs):
    refs[-1][...] = total[...].T


def place(half, total, grad, columns):
    size, width = total.shape
    in_specs = [pl.BlockSpec(memory_space=pltpu.VMEM)]
    args = [total]
    aliases = {}
    if grad is not None:
        in_specs.append(pl.BlockSpec(memory_space=pl.ANY))
        args.append(grad)
        aliases = {1: 0}
    return pl.pallas_call(
        place_kernel,
        grid=(1,),
        in_specs=in_specs,
        out_specs=pl.BlockSpec((width, size), lambda i: (0, half)),
        out_shape=jax.ShapeDtypeStruct((width, columns), jnp.float32),
        input_output_aliases=aliases,
        compiler_params=PARAMS,
        cost_estimate=SMALL,
        name="place",
    )(*args)


def reduce_on_grid(features, halves, firsts, attended, dp):
    width = features.shape[1] // dp
    columns = 2 * halves[0].shape[0]
    rank = lax.axis_index("dp")
    edge = (rank < 2) | (rank >= 6)

    def across(x):
        return lax.ppermute(x, "dp", [(r, r ^ 1) for r in range(dp)])

    def pair(x):
        return lax.ppermute(x, "dp", [(r, r ^ 2) for r in range(dp)])

    def outward(x):
        return lax.ppermute(x, "dp", [(r, r ^ 2) for r in (0, 1, 6, 7)])

    def inward(x):
        return lax.ppermute(x, "dp", [(r, r ^ 2) for r in (2, 3, 4, 5)])

    def middle(x):
        return lax.ppermute(x, "dp", [(r, r ^ 6) for r in (2, 3, 4, 5)])

    def together(*arrays):
        return lax.optimization_barrier(arrays)

    def after(x, *others):
        return together(x, *others)[0]

    def make(*jobs):
        return chunks(jobs, features, halves, width)

    a, b = 0, 1
    edge0, cross3a, cross3b = firsts
    (own3a, own3b, cross2a, cross2b, own2a, own2b, crosspb, crossoa, crossob, ownpa, ownpb, ownoa, ownob) = (
        make(
            ((FAR3, SAME), (a, b)),
            ((FAR2, CROSS), (a, b)),
            ((FAR2, SAME), (a, b)),
            ((PAIR, CROSS), (b,)),
            ((OWN, CROSS), (a, b)),
            ((PAIR, SAME), (a, b)),
            ((OWN, SAME), (a, b)),
        )
    )

    size = ownpa.shape[0]
    cut = size // EARLY
    e0 = pair(edge0)
    y0 = across(cross3a)
    y1 = after(across(cross3b), y0, e0)
    e2 = after(outward(own3a + y0), y1)
    y2 = after(across(after(cross2a, y0)), e2)
    e3 = after(outward(own3b + y1), y2)
    m3 = middle(own3a + y0 + e2)
    y3 = after(across(after(cross2b, y1, attended)), e3)
    e4 = after(outward(own2a + y2), y3)
    m4 = middle(own3b + y1 + e3)
    y4 = after(across(after(crosspb, y2)), e4)
    e5 = after(pair(jnp.where(edge, own2b + y3, ownpa + m3)), y4)
    m5 = middle(own2a + y2 + e4)
    y5 = across(after(jnp.concatenate([crossoa + e0[:size], crossob], axis=0), y3))
    late = outward(ownpa[cut:])
    e6 = pair(ownpb + y4 + m4)
    m6 = middle(own2b + y3 + e5)
    peaks = jnp.zeros((8, HD), jnp.float32)
    total, peaks = add_parts(a, cut, [ownoa, y5, m5, e0, late, e5], peaks)
    grad, peaks = together(place(a, total, None, columns), peaks)
    total, peaks = add_parts(b, cut, [ownob, y5, m6, e6], peaks)
    grad = place(b, total, grad, columns)
    for hop in (1, 2, 4):
        peaks = jnp.maximum(
            peaks, lax.ppermute(peaks, "dp", [(r, r ^ hop) for r in range(dp)])
        )
    return attended, grad, peaks[0, : columns // BUCKET]


def reduce_plain(features, halves):
    cots = jnp.concatenate(halves, axis=0)
    partial_grad = lax.dot_general(
        features, cots, (((0,), (1,)), ((), ())), preferred_element_type=jnp.float32
    )
    grad = lax.psum_scatter(partial_grad, "dp", scatter_dimension=0, tiled=True)
    peaks = jnp.max(jnp.abs(grad).reshape(-1, cots.shape[0] // BUCKET, BUCKET), axis=(0, 2))
    return grad, lax.pmax(peaks, "dp")


def per_device(
    dp,
    queries,
    cache_keys,
    cache_values,
    new_keys,
    new_values,
    features,
    cotangent,
    rewards,
    lengths,
):
    flat = features.reshape(-1, features.shape[2])
    arrays = (lengths, rewards, queries, cache_keys, new_keys, cotangent)
    on_grid = dp == 8
    width = features.shape[2] // 8 if on_grid else BUCKET
    half = cache_keys.shape[2] // 2
    jobs_a, jobs_b = (), ()
    if on_grid:
        jobs_a = (
            (((PAIR, CROSS), half), ((PAIR, SAME), half // EARLY)),
            (((FAR3, CROSS), half),),
        )
        jobs_b = ((((FAR3, CROSS), half),),)
    half_a, *firsts = begin(0, jobs_a, arrays, flat, width)
    half_b, *seconds = begin(1, jobs_b, arrays, flat, width)
    attended = attend(lengths, queries, cache_keys, new_keys, cache_values, new_values)
    firsts += seconds
    if on_grid:
        attended, grad, peaks = reduce_on_grid(
            flat, (half_a, half_b), firsts, attended, dp
        )
    else:
        grad, peaks = reduce_plain(flat, (half_a, half_b))
    return attended, grad, peaks


def solution(mesh):
    split = P(("groups", "dp"), None, "tensor")
    rows = P(("groups", "dp"))
    in_specs = (
        split,
        split,
        split,
        split,
        split,
        P(("groups", "dp"), None, None),
        split,
        rows,
        rows,
    )
    out_specs = (split, P(("groups", "dp"), "tensor"), P(("groups", "tensor")))
    return jax.shard_map(
        functools.partial(per_device, mesh.shape["dp"]),
        mesh=mesh,
        in_specs=in_specs,
        out_specs=out_specs,
        check_vma=False,
    )
```

```python
import functools
import math

import jax
import jax.numpy as jnp
from jax import lax
from jax.experimental import pallas as pl
from jax.experimental.pallas import tpu as pltpu
from jax.sharding import PartitionSpec as P

HD = 128
GROUP = 8
BUCKET = 128
BATCH = 16
EARLY = 2
VMEM_BYTES = 20 * 1024 * 1024
HBM = pl.BlockSpec(memory_space=pltpu.HBM)
PARAMS = pltpu.CompilerParams(vmem_limit_bytes=VMEM_BYTES)
MIDDLE = pltpu.CompilerParams(vmem_limit_bytes=46 * 1024 * 1024)
WIDE = pltpu.CompilerParams(vmem_limit_bytes=60 * 1024 * 1024)
SMALL = pl.CostEstimate(flops=1000, bytes_accessed=1000, transcendentals=0)
FAR3, FAR2, PAIR, OWN = range(4)
CROSS, SAME = True, False


def advantage_rows(rewards):
    advantages = []
    for base in range(0, rewards.shape[0], GROUP):
        centre = rewards[base]
        for i in range(1, GROUP):
            centre = centre + rewards[base + i]
        centre = centre * (1.0 / GROUP)
        spread = (rewards[base] - centre) * (rewards[base] - centre)
        for i in range(1, GROUP):
            spread = spread + (rewards[base + i] - centre) * (rewards[base + i] - centre)
        spread = jnp.sqrt(jnp.full((1, HD), spread * (1.0 / GROUP), jnp.float32))
        spread = jnp.maximum(spread, 1.0)
        for r in range(base, base + GROUP):
            advantages.append(jnp.full((1, HD), rewards[r] - centre, jnp.float32) / spread)
    return advantages


def attend_heads(lengths, rewards, q, ck, nk, cv=None, nv=None, out=None, cot=None, rows=None):
    rollouts, steps, width = q.shape
    key_heads = ck.shape[2] // HD
    heads = width // HD // key_heads
    ctx = ck.shape[1]
    slots = ctx + steps
    padded = -(-slots // HD) * HD
    pad = padded - slots
    scaling = 1.0 / math.sqrt(HD)

    def by_head(ref, r, g):
        return jnp.concatenate(
            [
                ref[r, :, (g * heads + j) * HD : (g * heads + j + 1) * HD].astype(jnp.float32)
                for j in range(heads)
            ],
            axis=0,
        )

    def joined(past, fresh, r, g):
        lanes = slice(g * HD, (g + 1) * HD)
        fresh = jnp.concatenate(
            [fresh[r, :, lanes].astype(jnp.float32), jnp.zeros((pad, HD), jnp.float32)], axis=0
        ).astype(jnp.bfloat16)
        return jnp.concatenate([past[r, :, lanes], fresh], axis=0)

    shape = (heads * steps, padded)
    column = lax.broadcasted_iota(jnp.int32, shape, 1)
    step = lax.broadcasted_iota(jnp.int32, shape, 0) % steps
    fresh_live = (column >= ctx) & (column - ctx <= step)
    advantages = advantage_rows(rewards) if rows is not None else None
    lives = []
    for r in range(rollouts):
        lives.append((column < lengths[r]) | fresh_live)
    units = [(r, g) for g in range(key_heads) for r in range(rollouts)]
    for start in range(0, len(units), BATCH):
        batch = units[start : start + BATCH]
        scores = [
            lax.dot_general(
                by_head(q, r, g).astype(jnp.bfloat16),
                joined(ck, nk, r, g),
                (((1,), (1,)), ((), ())),
                preferred_element_type=jnp.float32,
            )
            for r, g in batch
        ]
        scores = [
            jnp.where(lives[r], x * scaling, -1e30) for (r, g), x in zip(batch, scores)
        ]
        highest = [jnp.max(x, axis=1, keepdims=True) for x in scores]
        lift = [jnp.exp(x - top) for x, top in zip(scores, highest)]
        totals = [jnp.sum(x, axis=1, keepdims=True) for x in lift]
        weights = [(x / total).astype(jnp.bfloat16) for x, total in zip(lift, totals)]
        if out is not None:
            results = [
                jnp.dot(w, joined(cv, nv, r, g), preferred_element_type=jnp.float32)
                for (r, g), w in zip(batch, weights)
            ]
            for (r, g), result in zip(batch, results):
                for j in range(heads):
                    out[r, :, (g * heads + j) * HD : (g * heads + j + 1) * HD] = result[
                        j * steps : (j + 1) * steps
                    ].astype(jnp.bfloat16)
        if rows is not None:
            value_cots = [
                lax.dot_general(
                    w,
                    (by_head(cot, r, g) * advantages[r]).astype(jnp.bfloat16),
                    (((0,), (0,)), ((), ())),
                    preferred_element_type=jnp.float32,
                )
                for (r, g), w in zip(batch, weights)
            ]
            for (r, g), value_cot in zip(batch, value_cots):
                rows[r * slots : (r + 1) * slots, g * HD : (g + 1) * HD] = value_cot[:slots]


def block_of(kind):
    plane_kind, cross = kind
    rank = lax.axis_index("dp")
    plane = rank // 2
    row = rank - plane * 2
    low = plane < 2
    if plane_kind == FAR3:
        target = jnp.where(low, 3, 0)
    elif plane_kind == FAR2:
        target = jnp.where(low, 2, 1)
    elif plane_kind == PAIR:
        target = plane + 1 - 2 * (plane - (plane // 2) * 2)
    else:
        target = plane
    return target * 2 + (1 - row if cross else row)


def start_features(features, kinds, buffers, sems):
    copies = []
    for i, kind in enumerate(kinds):
        width = buffers.shape[2]
        first = pl.multiple_of(block_of(kind) * width, HD)
        copy = pltpu.make_async_copy(
            features.at[:, pl.ds(first, width)], buffers.at[i], sems.at[i]
        )
        copy.start()
        copies.append(copy)
    return copies


def copy_all(sources, buffers, sems):
    copies = []
    for i, (source, buffer) in enumerate(zip(sources, buffers)):
        copy = pltpu.make_async_copy(source, buffer, sems.at[i])
        copy.start()
        copies.append(copy)
    return copies


def lanes_of(ref, half):
    size = ref.shape[-1] // 2
    return ref.at[:, :, pl.ds(half * size, size)]


def begin_kernel(half, jobs, *refs):
    ins, refs = refs[:6], refs[6:]
    features, refs = refs[0], refs[1:]
    cot_half, refs = refs[0], refs[1:]
    outs, refs = refs[: len(jobs)], refs[len(jobs) :]
    bufs, (rows, blocks, sems, block_sems) = refs[:6], refs[6:]
    sources = list(ins[:2]) + [lanes_of(ref, half) for ref in ins[2:]]
    copies = copy_all(sources, bufs, sems)
    kinds = [kind for job in jobs for kind, _ in job]
    block_copies = start_features(features, kinds, blocks, block_sems)
    for copy in copies:
        copy.wait()
    lengths, rewards, q, ck, nk, cot = bufs
    attend_heads(lengths, rewards, q, ck, nk, cot=cot, rows=rows)
    cots = rows[...].T.astype(jnp.bfloat16)
    cot_half[...] = cots
    place = 0
    for out, job in zip(outs, jobs):
        first = 0
        for _, size in job:
            block_copies[place].wait()
            out[first : first + size] = jnp.dot(
                cots[:size], blocks[place], preferred_element_type=jnp.float32
            )
            first += size
            place += 1


def begin(half, jobs, arrays, features, width):
    lengths, rewards, queries, ck, _, _ = arrays
    depth = features.shape[0]
    columns = ck.shape[2] // 2
    count = max(sum(len(job) for job in jobs), 1)
    shapes = [jax.ShapeDtypeStruct((columns, depth), jnp.bfloat16)]
    for job in jobs:
        shapes.append(jax.ShapeDtypeStruct((sum(size for _, size in job), width), jnp.float32))
    vmem = pl.BlockSpec(memory_space=pltpu.VMEM)
    return pl.pallas_call(
        functools.partial(begin_kernel, half, jobs),
        in_specs=[HBM] * 7,
        out_specs=[vmem] * len(shapes),
        out_shape=shapes,
        scratch_shapes=[pltpu.SMEM(x.shape, x.dtype) for x in arrays[:2]]
        + [pltpu.VMEM(x.shape[:2] + (x.shape[2] // 2,), x.dtype) for x in arrays[2:]]
        + [
            pltpu.VMEM((depth, columns), jnp.float32),
            pltpu.VMEM((count, depth, width), jnp.bfloat16),
            pltpu.SemaphoreType.DMA((6,)),
            pltpu.SemaphoreType.DMA((count,)),
        ],
        compiler_params=WIDE,
        cost_estimate=SMALL,
        name="value_cot",
    )(*arrays, features)


def attended_kernel(*refs):
    ins, out, bufs, sems = refs[:6], refs[6], refs[7:13], refs[13]
    for copy in copy_all(ins, bufs, sems):
        copy.wait()
    lengths, queries, ck, nk, cv, nv = bufs
    attend_heads(lengths, None, queries, ck, nk, cv=cv, nv=nv, out=out)


def attend(*arrays):
    queries = arrays[1]
    return pl.pallas_call(
        attended_kernel,
        in_specs=[HBM] * 6,
        out_specs=pl.BlockSpec(memory_space=pltpu.VMEM),
        out_shape=jax.ShapeDtypeStruct(queries.shape, jnp.bfloat16),
        scratch_shapes=[pltpu.SMEM(arrays[0].shape, arrays[0].dtype)]
        + [pltpu.VMEM(x.shape, x.dtype) for x in arrays[1:]]
        + [pltpu.SemaphoreType.DMA((6,))],
        compiler_params=MIDDLE,
        cost_estimate=SMALL,
        name="attend",
    )(*arrays)


def chunk_kernel(jobs, features, half_a, half_b, *refs):
    kinds = [kind for kind, _ in jobs]
    count = sum(len(which) for _, which in jobs)
    outs, (blocks, sems) = refs[:count], refs[count:]
    copies = start_features(features, kinds, blocks, sems)
    cots = (half_a, half_b)
    place = 0
    for i, (_, which) in enumerate(jobs):
        copies[i].wait()
        for h in which:
            outs[place][...] = jnp.dot(
                cots[h][...], blocks[i], preferred_element_type=jnp.float32
            )
            place += 1


def chunks(jobs, features, halves, width):
    depth = features.shape[0]
    half = halves[0].shape[0]
    count = sum(len(which) for _, which in jobs)
    vmem = pl.BlockSpec(memory_space=pltpu.VMEM)
    return pl.pallas_call(
        functools.partial(chunk_kernel, jobs),
        in_specs=[HBM, vmem, vmem],
        out_specs=[vmem] * count,
        out_shape=[jax.ShapeDtypeStruct((half, width), jnp.float32)] * count,
        scratch_shapes=[
            pltpu.VMEM((len(jobs), depth, width), jnp.bfloat16),
            pltpu.SemaphoreType.DMA((len(jobs),)),
        ],
        compiler_params=MIDDLE,
        cost_estimate=SMALL,
        name="chunk",
    )(features, *halves)


def add_kernel(*refs):
    own_a, own_b, cross, mid_a, mid_b, first, late, last_a, last_b, total, peaks = refs
    size = own_a.shape[0]
    rank = lax.axis_index("dp")
    edge = (rank < 2) | (rank >= 6)
    piece = jnp.concatenate([first[size:], late[...]], axis=0)
    arrived = jnp.where(edge, last_a[...], piece)
    total[:size] = own_a[...] + cross[:size] + mid_a[...] + arrived
    total[size:] = own_b[...] + cross[size:] + mid_b[...] + last_b[...]
    lane = lax.broadcasted_iota(jnp.int32, peaks.shape, 1)
    peak = jnp.zeros(peaks.shape, jnp.float32)
    for b in range(2 * size // BUCKET):
        top = jnp.abs(total[b * BUCKET : (b + 1) * BUCKET])
        top = jnp.max(jnp.max(top, axis=0, keepdims=True), axis=1, keepdims=True)
        peak = jnp.where(lane == b, top, peak)
    peaks[...] = peak


def add_parts(parts):
    vmem = pl.BlockSpec(memory_space=pltpu.VMEM)
    size, width = parts[0].shape
    return pl.pallas_call(
        add_kernel,
        in_specs=[vmem] * len(parts),
        out_specs=[vmem] * 2,
        out_shape=[
            jax.ShapeDtypeStruct((2 * size, width), jnp.float32),
            jax.ShapeDtypeStruct((8, HD), jnp.float32),
        ],
        compiler_params=PARAMS,
        cost_estimate=SMALL,
        name="add_parts",
    )(*parts)


def place_kernel(total, grad):
    grad[...] = total[...].T


def place(total):
    columns, width = total.shape
    vmem = pl.BlockSpec(memory_space=pltpu.VMEM)
    return pl.pallas_call(
        place_kernel,
        in_specs=[vmem],
        out_specs=vmem,
        out_shape=jax.ShapeDtypeStruct((width, columns), jnp.float32),
        compiler_params=PARAMS,
        cost_estimate=SMALL,
        name="place",
    )(total)


def reduce_on_grid(features, halves, firsts, attended, dp):
    width = features.shape[1] // dp
    columns = 2 * halves[0].shape[0]
    rank = lax.axis_index("dp")
    edge = (rank < 2) | (rank >= 6)

    def across(x):
        return lax.ppermute(x, "dp", [(r, r ^ 1) for r in range(dp)])

    def pair(x):
        return lax.ppermute(x, "dp", [(r, r ^ 2) for r in range(dp)])

    def outward(x):
        return lax.ppermute(x, "dp", [(r, r ^ 2) for r in (0, 1, 6, 7)])

    def inward(x):
        return lax.ppermute(x, "dp", [(r, r ^ 2) for r in (2, 3, 4, 5)])

    def middle(x):
        return lax.ppermute(x, "dp", [(r, r ^ 6) for r in (2, 3, 4, 5)])

    def together(*arrays):
        return lax.optimization_barrier(arrays)

    def after(x, *others):
        return together(x, *others)[0]

    def make(*jobs):
        return chunks(jobs, features, halves, width)

    a, b = 0, 1
    edge0, cross3a, cross3b = firsts
    (own3a, own3b, cross2a, cross2b, own2a, own2b, crosspb, crossoa, crossob, ownpa, ownpb, ownoa, ownob) = (
        make(
            ((FAR3, SAME), (a, b)),
            ((FAR2, CROSS), (a, b)),
            ((FAR2, SAME), (a, b)),
            ((PAIR, CROSS), (b,)),
            ((OWN, CROSS), (a, b)),
            ((PAIR, SAME), (a, b)),
            ((OWN, SAME), (a, b)),
        )
    )

    size = ownpa.shape[0]
    cut = size // EARLY
    e0 = pair(edge0)
    y0 = across(cross3a)
    y1 = after(across(cross3b), y0, e0)
    e2 = after(outward(own3a + y0), y1)
    y2 = after(across(after(cross2a, y0)), e2)
    e3 = after(outward(own3b + y1), y2)
    m3 = middle(own3a + y0 + e2)
    y3 = after(across(after(cross2b, y1, attended)), e3)
    e4 = after(outward(own2a + y2), y3)
    m4 = middle(own3b + y1 + e3)
    y4 = after(across(after(crosspb, y2)), e4)
    e5 = after(pair(jnp.where(edge, own2b + y3, ownpa + m3)), y4)
    m5 = middle(own2a + y2 + e4)
    y5 = across(after(jnp.concatenate([crossoa + e0[:size], crossob], axis=0), y3))
    late = outward(after(ownpa[cut:], m5))
    e6 = pair(ownpb + y4 + m4)
    m6 = middle(own2b + y3 + e5)
    total, peaks = add_parts([ownoa, ownob, y5, m5, m6, e0, late, e5, e6])
    peaks = jnp.maximum(peaks, across(peaks))
    peaks, grad = together(jnp.maximum(peaks, pair(peaks)), place(total))
    peaks = jnp.maximum(peaks, lax.ppermute(peaks, "dp", [(r, r ^ 4) for r in range(dp)]))
    return attended, grad, peaks[0, : columns // BUCKET]


def reduce_plain(features, halves):
    cots = jnp.concatenate(halves, axis=0)
    partial_grad = lax.dot_general(
        features, cots, (((0,), (1,)), ((), ())), preferred_element_type=jnp.float32
    )
    grad = lax.psum_scatter(partial_grad, "dp", scatter_dimension=0, tiled=True)
    peaks = jnp.max(jnp.abs(grad).reshape(-1, cots.shape[0] // BUCKET, BUCKET), axis=(0, 2))
    return grad, lax.pmax(peaks, "dp")


def per_device(
    dp,
    queries,
    cache_keys,
    cache_values,
    new_keys,
    new_values,
    features,
    cotangent,
    rewards,
    lengths,
):
    flat = features.reshape(-1, features.shape[2])
    arrays = (lengths, rewards, queries, cache_keys, new_keys, cotangent)
    on_grid = dp == 8
    width = features.shape[2] // 8 if on_grid else BUCKET
    half = cache_keys.shape[2] // 2
    jobs_a, jobs_b = (), ()
    if on_grid:
        jobs_a = (
            (((PAIR, CROSS), half), ((PAIR, SAME), half // EARLY)),
            (((FAR3, CROSS), half),),
        )
        jobs_b = ((((FAR3, CROSS), half),),)
    half_a, *firsts = begin(0, jobs_a, arrays, flat, width)
    half_b, *seconds = begin(1, jobs_b, arrays, flat, width)
    attended = attend(lengths, queries, cache_keys, new_keys, cache_values, new_values)
    firsts += seconds
    if on_grid:
        attended, grad, peaks = reduce_on_grid(
            flat, (half_a, half_b), firsts, attended, dp
        )
    else:
        grad, peaks = reduce_plain(flat, (half_a, half_b))
    return attended, grad, peaks


def solution(mesh):
    split = P(("groups", "dp"), None, "tensor")
    rows = P(("groups", "dp"))
    in_specs = (
        split,
        split,
        split,
        split,
        split,
        P(("groups", "dp"), None, None),
        split,
        rows,
        rows,
    )
    out_specs = (split, P(("groups", "dp"), "tensor"), P(("groups", "tensor")))
    return jax.shard_map(
        functools.partial(per_device, mesh.shape["dp"]),
        mesh=mesh,
        in_specs=in_specs,
        out_specs=out_specs,
        check_vma=False,
    )
```

```python
import functools
import math

import jax
import jax.numpy as jnp
from jax import lax
from jax.experimental import pallas as pl
from jax.experimental.pallas import tpu as pltpu
from jax.sharding import PartitionSpec as P

HD = 128
GROUP = 8
BUCKET = 128
BATCH = 16
EARLY = 2
VMEM_BYTES = 20 * 1024 * 1024
HBM = pl.BlockSpec(memory_space=pltpu.HBM)
PARAMS = pltpu.CompilerParams(vmem_limit_bytes=VMEM_BYTES)
MIDDLE = pltpu.CompilerParams(vmem_limit_bytes=46 * 1024 * 1024)
WIDE = pltpu.CompilerParams(vmem_limit_bytes=60 * 1024 * 1024)
SMALL = pl.CostEstimate(flops=1000, bytes_accessed=1000, transcendentals=0)
FAR3, FAR2, PAIR, OWN = range(4)
CROSS, SAME = True, False


def advantage_rows(rewards):
    advantages = []
    for base in range(0, rewards.shape[0], GROUP):
        centre = rewards[base]
        for i in range(1, GROUP):
            centre = centre + rewards[base + i]
        centre = centre * (1.0 / GROUP)
        spread = (rewards[base] - centre) * (rewards[base] - centre)
        for i in range(1, GROUP):
            spread = spread + (rewards[base + i] - centre) * (rewards[base + i] - centre)
        spread = jnp.sqrt(jnp.full((1, HD), spread * (1.0 / GROUP), jnp.float32))
        spread = jnp.maximum(spread, 1.0)
        for r in range(base, base + GROUP):
            advantages.append(jnp.full((1, HD), rewards[r] - centre, jnp.float32) / spread)
    return advantages


def attend_heads(lengths, rewards, q, ck, nk, cv=None, nv=None, out=None, cot=None, rows=None):
    rollouts, steps, width = q.shape
    key_heads = ck.shape[2] // HD
    heads = width // HD // key_heads
    ctx = ck.shape[1]
    slots = ctx + steps
    padded = -(-slots // HD) * HD
    pad = padded - slots
    scaling = 1.0 / math.sqrt(HD)

    def by_head(ref, r, g):
        return jnp.concatenate(
            [
                ref[r, :, (g * heads + j) * HD : (g * heads + j + 1) * HD].astype(jnp.float32)
                for j in range(heads)
            ],
            axis=0,
        )

    def joined(past, fresh, r, g):
        lanes = slice(g * HD, (g + 1) * HD)
        fresh = jnp.concatenate(
            [fresh[r, :, lanes].astype(jnp.float32), jnp.zeros((pad, HD), jnp.float32)], axis=0
        ).astype(jnp.bfloat16)
        return jnp.concatenate([past[r, :, lanes], fresh], axis=0)

    shape = (heads * steps, padded)
    column = lax.broadcasted_iota(jnp.int32, shape, 1)
    step = lax.broadcasted_iota(jnp.int32, shape, 0) % steps
    fresh_live = (column >= ctx) & (column - ctx <= step)
    advantages = advantage_rows(rewards) if rows is not None else None
    lives = []
    for r in range(rollouts):
        lives.append((column < lengths[r]) | fresh_live)
    units = [(r, g) for g in range(key_heads) for r in range(rollouts)]
    for start in range(0, len(units), BATCH):
        batch = units[start : start + BATCH]
        scores = [
            lax.dot_general(
                by_head(q, r, g).astype(jnp.bfloat16),
                joined(ck, nk, r, g),
                (((1,), (1,)), ((), ())),
                preferred_element_type=jnp.float32,
            )
            for r, g in batch
        ]
        scores = [
            jnp.where(lives[r], x * scaling, -1e30) for (r, g), x in zip(batch, scores)
        ]
        highest = [jnp.max(x, axis=1, keepdims=True) for x in scores]
        lift = [jnp.exp(x - top) for x, top in zip(scores, highest)]
        totals = [jnp.sum(x, axis=1, keepdims=True) for x in lift]
        weights = [(x / total).astype(jnp.bfloat16) for x, total in zip(lift, totals)]
        if out is not None:
            results = [
                jnp.dot(w, joined(cv, nv, r, g), preferred_element_type=jnp.float32)
                for (r, g), w in zip(batch, weights)
            ]
            for (r, g), result in zip(batch, results):
                for j in range(heads):
                    out[r, :, (g * heads + j) * HD : (g * heads + j + 1) * HD] = result[
                        j * steps : (j + 1) * steps
                    ].astype(jnp.bfloat16)
        if rows is not None:
            value_cots = [
                lax.dot_general(
                    w,
                    (by_head(cot, r, g) * advantages[r]).astype(jnp.bfloat16),
                    (((0,), (0,)), ((), ())),
                    preferred_element_type=jnp.float32,
                )
                for (r, g), w in zip(batch, weights)
            ]
            for (r, g), value_cot in zip(batch, value_cots):
                rows[r * slots : (r + 1) * slots, g * HD : (g + 1) * HD] = value_cot[:slots]


def block_of(kind):
    plane_kind, cross = kind
    rank = lax.axis_index("dp")
    plane = rank // 2
    row = rank - plane * 2
    low = plane < 2
    if plane_kind == FAR3:
        target = jnp.where(low, 3, 0)
    elif plane_kind == FAR2:
        target = jnp.where(low, 2, 1)
    elif plane_kind == PAIR:
        target = plane + 1 - 2 * (plane - (plane // 2) * 2)
    else:
        target = plane
    return target * 2 + (1 - row if cross else row)


def start_features(features, kinds, buffers, sems):
    copies = []
    for i, kind in enumerate(kinds):
        width = buffers.shape[2]
        first = pl.multiple_of(block_of(kind) * width, HD)
        copy = pltpu.make_async_copy(
            features.at[:, pl.ds(first, width)], buffers.at[i], sems.at[i]
        )
        copy.start()
        copies.append(copy)
    return copies


def copy_all(sources, buffers, sems):
    copies = []
    for i, (source, buffer) in enumerate(zip(sources, buffers)):
        copy = pltpu.make_async_copy(source, buffer, sems.at[i])
        copy.start()
        copies.append(copy)
    return copies


def lanes_of(ref, half):
    size = ref.shape[-1] // 2
    return ref.at[:, :, pl.ds(half * size, size)]


def begin_kernel(half, jobs, *refs):
    ins, refs = refs[:6], refs[6:]
    features, refs = refs[0], refs[1:]
    cot_half, refs = refs[0], refs[1:]
    outs, refs = refs[: len(jobs)], refs[len(jobs) :]
    bufs, (rows, blocks, sems, block_sems) = refs[:6], refs[6:]
    sources = list(ins[:2]) + [lanes_of(ref, half) for ref in ins[2:]]
    copies = copy_all(sources, bufs, sems)
    kinds = [kind for job in jobs for kind, _ in job]
    block_copies = start_features(features, kinds, blocks, block_sems)
    for copy in copies:
        copy.wait()
    lengths, rewards, q, ck, nk, cot = bufs
    attend_heads(lengths, rewards, q, ck, nk, cot=cot, rows=rows)
    cots = rows[...].T.astype(jnp.bfloat16)
    cot_half[...] = cots
    place = 0
    for out, job in zip(outs, jobs):
        first = 0
        for _, size in job:
            block_copies[place].wait()
            out[first : first + size] = jnp.dot(
                cots[:size], blocks[place], preferred_element_type=jnp.float32
            )
            first += size
            place += 1


def begin(half, jobs, arrays, features, width):
    lengths, rewards, queries, ck, _, _ = arrays
    depth = features.shape[0]
    columns = ck.shape[2] // 2
    count = max(sum(len(job) for job in jobs), 1)
    shapes = [jax.ShapeDtypeStruct((columns, depth), jnp.bfloat16)]
    for job in jobs:
        shapes.append(jax.ShapeDtypeStruct((sum(size for _, size in job), width), jnp.float32))
    vmem = pl.BlockSpec(memory_space=pltpu.VMEM)
    return pl.pallas_call(
        functools.partial(begin_kernel, half, jobs),
        in_specs=[HBM] * 7,
        out_specs=[vmem] * len(shapes),
        out_shape=shapes,
        scratch_shapes=[pltpu.SMEM(x.shape, x.dtype) for x in arrays[:2]]
        + [pltpu.VMEM(x.shape[:2] + (x.shape[2] // 2,), x.dtype) for x in arrays[2:]]
        + [
            pltpu.VMEM((depth, columns), jnp.float32),
            pltpu.VMEM((count, depth, width), jnp.bfloat16),
            pltpu.SemaphoreType.DMA((6,)),
            pltpu.SemaphoreType.DMA((count,)),
        ],
        compiler_params=WIDE,
        cost_estimate=SMALL,
        name="value_cot",
    )(*arrays, features)


def attended_kernel(*refs):
    ins, out, bufs, sems = refs[:6], refs[6], refs[7:13], refs[13]
    for copy in copy_all(ins, bufs, sems):
        copy.wait()
    lengths, queries, ck, nk, cv, nv = bufs
    attend_heads(lengths, None, queries, ck, nk, cv=cv, nv=nv, out=out)


def attend(*arrays):
    queries = arrays[1]
    return pl.pallas_call(
        attended_kernel,
        in_specs=[HBM] * 6,
        out_specs=pl.BlockSpec(memory_space=pltpu.VMEM),
        out_shape=jax.ShapeDtypeStruct(queries.shape, jnp.bfloat16),
        scratch_shapes=[pltpu.SMEM(arrays[0].shape, arrays[0].dtype)]
        + [pltpu.VMEM(x.shape, x.dtype) for x in arrays[1:]]
        + [pltpu.SemaphoreType.DMA((6,))],
        compiler_params=MIDDLE,
        cost_estimate=SMALL,
        name="attend",
    )(*arrays)


def chunk_kernel(jobs, features, half_a, half_b, *refs):
    kinds = [kind for kind, _ in jobs]
    count = sum(len(which) for _, which in jobs)
    outs, (blocks, sems) = refs[:count], refs[count:]
    copies = start_features(features, kinds, blocks, sems)
    cots = (half_a, half_b)
    place = 0
    for i, (_, which) in enumerate(jobs):
        copies[i].wait()
        for h in which:
            outs[place][...] = jnp.dot(
                cots[h][...], blocks[i], preferred_element_type=jnp.float32
            )
            place += 1


def chunks(jobs, features, halves, width):
    depth = features.shape[0]
    half = halves[0].shape[0]
    count = sum(len(which) for _, which in jobs)
    vmem = pl.BlockSpec(memory_space=pltpu.VMEM)
    return pl.pallas_call(
        functools.partial(chunk_kernel, jobs),
        in_specs=[HBM, vmem, vmem],
        out_specs=[vmem] * count,
        out_shape=[jax.ShapeDtypeStruct((half, width), jnp.float32)] * count,
        scratch_shapes=[
            pltpu.VMEM((len(jobs), depth, width), jnp.bfloat16),
            pltpu.SemaphoreType.DMA((len(jobs),)),
        ],
        compiler_params=MIDDLE,
        cost_estimate=SMALL,
        name="chunk",
    )(features, *halves)


def add_kernel(*refs):
    own_a, own_b, cross, mid_a, mid_b, first, late, last_a, last_b, total, peaks = refs
    size = own_a.shape[0]
    rank = lax.axis_index("dp")
    edge = (rank < 2) | (rank >= 6)
    piece = jnp.concatenate([first[size:], late[...]], axis=0)
    arrived = jnp.where(edge, last_a[...], piece)
    total[:size] = own_a[...] + cross[:size] + mid_a[...] + arrived
    total[size:] = own_b[...] + cross[size:] + mid_b[...] + last_b[...]
    lane = lax.broadcasted_iota(jnp.int32, peaks.shape, 1)
    peak = jnp.zeros(peaks.shape, jnp.float32)
    for b in range(2 * size // BUCKET):
        top = jnp.abs(total[b * BUCKET : (b + 1) * BUCKET])
        top = jnp.max(jnp.max(top, axis=0, keepdims=True), axis=1, keepdims=True)
        peak = jnp.where(lane == b, top, peak)
    peaks[...] = peak


def add_parts(parts):
    vmem = pl.BlockSpec(memory_space=pltpu.VMEM)
    size, width = parts[0].shape
    return pl.pallas_call(
        add_kernel,
        in_specs=[vmem] * len(parts),
        out_specs=[vmem] * 2,
        out_shape=[
            jax.ShapeDtypeStruct((2 * size, width), jnp.float32),
            jax.ShapeDtypeStruct((8, HD), jnp.float32),
        ],
        compiler_params=PARAMS,
        cost_estimate=SMALL,
        name="add_parts",
    )(*parts)


def place_kernel(total, grad):
    grad[...] = total[...].T


def place(total):
    columns, width = total.shape
    vmem = pl.BlockSpec(memory_space=pltpu.VMEM)
    return pl.pallas_call(
        place_kernel,
        in_specs=[vmem],
        out_specs=vmem,
        out_shape=jax.ShapeDtypeStruct((width, columns), jnp.float32),
        compiler_params=PARAMS,
        cost_estimate=SMALL,
        name="place",
    )(total)


def reduce_on_grid(features, halves, firsts, attended, dp):
    width = features.shape[1] // dp
    columns = 2 * halves[0].shape[0]
    rank = lax.axis_index("dp")
    edge = (rank < 2) | (rank >= 6)

    def across(x):
        return lax.ppermute(x, "dp", [(r, r ^ 1) for r in range(dp)])

    def pair(x):
        return lax.ppermute(x, "dp", [(r, r ^ 2) for r in range(dp)])

    def outward(x):
        return lax.ppermute(x, "dp", [(r, r ^ 2) for r in (0, 1, 6, 7)])

    def inward(x):
        return lax.ppermute(x, "dp", [(r, r ^ 2) for r in (2, 3, 4, 5)])

    def middle(x):
        return lax.ppermute(x, "dp", [(r, r ^ 6) for r in (2, 3, 4, 5)])

    def together(*arrays):
        return lax.optimization_barrier(arrays)

    def after(x, *others):
        return together(x, *others)[0]

    def planes(x, hop):
        return lax.ppermute(x, "dp", [(r, r ^ hop) for r in range(dp)])

    def make(*jobs):
        return chunks(jobs, features, halves, width)

    a, b = 0, 1
    edge0, cross3a, cross3b = firsts
    (own3a, own3b, cross2a, cross2b, own2a, own2b, crosspb, crossoa, crossob, ownpa, ownpb, ownoa, ownob) = (
        make(
            ((FAR3, SAME), (a, b)),
            ((FAR2, CROSS), (a, b)),
            ((FAR2, SAME), (a, b)),
            ((PAIR, CROSS), (b,)),
            ((OWN, CROSS), (a, b)),
            ((PAIR, SAME), (a, b)),
            ((OWN, SAME), (a, b)),
        )
    )

    size = ownpa.shape[0]
    cut = size // EARLY
    e0 = pair(edge0)
    y0 = across(cross3a)
    y1 = after(across(cross3b), y0, e0)
    e2 = after(outward(own3a + y0), y1)
    y2 = after(across(after(cross2a, y0)), e2)
    e3 = after(outward(own3b + y1), y2)
    m3 = middle(own3a + y0 + e2)
    y3 = after(across(after(cross2b, y1, attended)), e3)
    e4 = after(outward(own2a + y2), y3)
    m4 = middle(own3b + y1 + e3)
    y4 = after(across(after(crosspb, y2)), e4)
    e5 = after(pair(jnp.where(edge, own2b + y3, ownpa + m3)), y4)
    m5 = middle(own2a + y2 + e4)
    y5 = across(after(jnp.concatenate([crossoa + e0[:size], crossob], axis=0), y3))
    late = outward(after(ownpa[cut:], m5))
    e6 = pair(ownpb + y4 + m4)
    m6 = middle(own2b + y3 + e5)
    total, peaks = add_parts([ownoa, ownob, y5, m5, m6, e0, late, e5, e6])
    peaks, grad = together(jnp.maximum(peaks, across(peaks)), place(total))
    near, far, middle_peaks = [planes(peaks, hop) for hop in (2, 4, 6)]
    peaks = jnp.maximum(jnp.maximum(peaks, near), jnp.maximum(far, middle_peaks))
    return attended, grad, peaks[0, : columns // BUCKET]


def reduce_plain(features, halves):
    cots = jnp.concatenate(halves, axis=0)
    partial_grad = lax.dot_general(
        features, cots, (((0,), (1,)), ((), ())), preferred_element_type=jnp.float32
    )
    grad = lax.psum_scatter(partial_grad, "dp", scatter_dimension=0, tiled=True)
    peaks = jnp.max(jnp.abs(grad).reshape(-1, cots.shape[0] // BUCKET, BUCKET), axis=(0, 2))
    return grad, lax.pmax(peaks, "dp")


def per_device(
    dp,
    queries,
    cache_keys,
    cache_values,
    new_keys,
    new_values,
    features,
    cotangent,
    rewards,
    lengths,
):
    flat = features.reshape(-1, features.shape[2])
    arrays = (lengths, rewards, queries, cache_keys, new_keys, cotangent)
    on_grid = dp == 8
    width = features.shape[2] // 8 if on_grid else BUCKET
    half = cache_keys.shape[2] // 2
    jobs_a, jobs_b = (), ()
    if on_grid:
        jobs_a = (
            (((PAIR, CROSS), half), ((PAIR, SAME), half // EARLY)),
            (((FAR3, CROSS), half),),
        )
        jobs_b = ((((FAR3, CROSS), half),),)
    half_a, *firsts = begin(0, jobs_a, arrays, flat, width)
    half_b, *seconds = begin(1, jobs_b, arrays, flat, width)
    attended = attend(lengths, queries, cache_keys, new_keys, cache_values, new_values)
    firsts += seconds
    if on_grid:
        attended, grad, peaks = reduce_on_grid(
            flat, (half_a, half_b), firsts, attended, dp
        )
    else:
        grad, peaks = reduce_plain(flat, (half_a, half_b))
    return attended, grad, peaks


def solution(mesh):
    split = P(("groups", "dp"), None, "tensor")
    rows = P(("groups", "dp"))
    in_specs = (
        split,
        split,
        split,
        split,
        split,
        P(("groups", "dp"), None, None),
        split,
        rows,
        rows,
    )
    out_specs = (split, P(("groups", "dp"), "tensor"), P(("groups", "tensor")))
    return jax.shard_map(
        functools.partial(per_device, mesh.shape["dp"]),
        mesh=mesh,
        in_specs=in_specs,
        out_specs=out_specs,
        check_vma=False,
    )
```

```python
import functools
import math

import jax
import jax.numpy as jnp
from jax import lax
from jax.experimental import pallas as pl
from jax.experimental.pallas import tpu as pltpu
from jax.sharding import PartitionSpec as P

HD = 128
GROUP = 8
BUCKET = 128
BATCH = 16
EARLY = 2
VMEM_BYTES = 20 * 1024 * 1024
HBM = pl.BlockSpec(memory_space=pltpu.HBM)
PARAMS = pltpu.CompilerParams(vmem_limit_bytes=VMEM_BYTES)
MIDDLE = pltpu.CompilerParams(vmem_limit_bytes=46 * 1024 * 1024)
WIDE = pltpu.CompilerParams(vmem_limit_bytes=60 * 1024 * 1024)
SMALL = pl.CostEstimate(flops=1000, bytes_accessed=1000, transcendentals=0)
FAR3, FAR2, PAIR, OWN = range(4)
CROSS, SAME = True, False


def advantage_rows(rewards):
    advantages = []
    for base in range(0, rewards.shape[0], GROUP):
        centre = rewards[base]
        for i in range(1, GROUP):
            centre = centre + rewards[base + i]
        centre = centre * (1.0 / GROUP)
        spread = (rewards[base] - centre) * (rewards[base] - centre)
        for i in range(1, GROUP):
            spread = spread + (rewards[base + i] - centre) * (rewards[base + i] - centre)
        spread = jnp.sqrt(jnp.full((1, HD), spread * (1.0 / GROUP), jnp.float32))
        spread = jnp.maximum(spread, 1.0)
        for r in range(base, base + GROUP):
            advantages.append(jnp.full((1, HD), rewards[r] - centre, jnp.float32) / spread)
    return advantages


def attend_heads(lengths, rewards, q, ck, nk, cv=None, nv=None, out=None, cot=None, rows=None):
    rollouts, steps, width = q.shape
    key_heads = ck.shape[2] // HD
    heads = width // HD // key_heads
    ctx = ck.shape[1]
    slots = ctx + steps
    padded = -(-slots // HD) * HD
    pad = padded - slots
    scaling = 1.0 / math.sqrt(HD)

    def by_head(ref, r, g):
        return jnp.concatenate(
            [
                ref[r, :, (g * heads + j) * HD : (g * heads + j + 1) * HD].astype(jnp.float32)
                for j in range(heads)
            ],
            axis=0,
        )

    def joined(past, fresh, r, g):
        lanes = slice(g * HD, (g + 1) * HD)
        fresh = jnp.concatenate(
            [fresh[r, :, lanes].astype(jnp.float32), jnp.zeros((pad, HD), jnp.float32)], axis=0
        ).astype(jnp.bfloat16)
        return jnp.concatenate([past[r, :, lanes], fresh], axis=0)

    shape = (heads * steps, padded)
    column = lax.broadcasted_iota(jnp.int32, shape, 1)
    step = lax.broadcasted_iota(jnp.int32, shape, 0) % steps
    fresh_live = (column >= ctx) & (column - ctx <= step)
    advantages = advantage_rows(rewards) if rows is not None else None
    lives = []
    for r in range(rollouts):
        lives.append((column < lengths[r]) | fresh_live)
    units = [(r, g) for g in range(key_heads) for r in range(rollouts)]
    for start in range(0, len(units), BATCH):
        batch = units[start : start + BATCH]
        scores = [
            lax.dot_general(
                by_head(q, r, g).astype(jnp.bfloat16),
                joined(ck, nk, r, g),
                (((1,), (1,)), ((), ())),
                preferred_element_type=jnp.float32,
            )
            for r, g in batch
        ]
        scores = [
            jnp.where(lives[r], x * scaling, -1e30) for (r, g), x in zip(batch, scores)
        ]
        highest = [jnp.max(x, axis=1, keepdims=True) for x in scores]
        lift = [jnp.exp(x - top) for x, top in zip(scores, highest)]
        totals = [jnp.sum(x, axis=1, keepdims=True) for x in lift]
        weights = [(x / total).astype(jnp.bfloat16) for x, total in zip(lift, totals)]
        if out is not None:
            results = [
                jnp.dot(w, joined(cv, nv, r, g), preferred_element_type=jnp.float32)
                for (r, g), w in zip(batch, weights)
            ]
            for (r, g), result in zip(batch, results):
                for j in range(heads):
                    out[r, :, (g * heads + j) * HD : (g * heads + j + 1) * HD] = result[
                        j * steps : (j + 1) * steps
                    ].astype(jnp.bfloat16)
        if rows is not None:
            value_cots = [
                lax.dot_general(
                    w,
                    (by_head(cot, r, g) * advantages[r]).astype(jnp.bfloat16),
                    (((0,), (0,)), ((), ())),
                    preferred_element_type=jnp.float32,
                )
                for (r, g), w in zip(batch, weights)
            ]
            for (r, g), value_cot in zip(batch, value_cots):
                rows[r * slots : (r + 1) * slots, g * HD : (g + 1) * HD] = value_cot[:slots]


def block_of(kind):
    plane_kind, cross = kind
    rank = lax.axis_index("dp")
    plane = rank // 2
    row = rank - plane * 2
    low = plane < 2
    if plane_kind == FAR3:
        target = jnp.where(low, 3, 0)
    elif plane_kind == FAR2:
        target = jnp.where(low, 2, 1)
    elif plane_kind == PAIR:
        target = plane + 1 - 2 * (plane - (plane // 2) * 2)
    else:
        target = plane
    return target * 2 + (1 - row if cross else row)


def start_features(features, kinds, buffers, sems):
    copies = []
    for i, kind in enumerate(kinds):
        width = buffers.shape[2]
        first = pl.multiple_of(block_of(kind) * width, HD)
        copy = pltpu.make_async_copy(
            features.at[:, pl.ds(first, width)], buffers.at[i], sems.at[i]
        )
        copy.start()
        copies.append(copy)
    return copies


def copy_all(sources, buffers, sems):
    copies = []
    for i, (source, buffer) in enumerate(zip(sources, buffers)):
        copy = pltpu.make_async_copy(source, buffer, sems.at[i])
        copy.start()
        copies.append(copy)
    return copies


def lanes_of(ref, half):
    size = ref.shape[-1] // 2
    return ref.at[:, :, pl.ds(half * size, size)]


def begin_kernel(half, jobs, *refs):
    ins, refs = refs[:6], refs[6:]
    features, refs = refs[0], refs[1:]
    cot_half, refs = refs[0], refs[1:]
    outs, refs = refs[: len(jobs)], refs[len(jobs) :]
    bufs, (rows, blocks, both, sems, block_sems) = refs[:6], refs[6:]
    sources = list(ins[:2]) + [lanes_of(ref, half) for ref in ins[2:]]
    copies = copy_all(sources, bufs, sems)
    kinds = [kind for job in jobs for kind, _ in job]
    width = blocks.shape[2]
    joined = kinds[:2] == [(PAIR, CROSS), (PAIR, SAME)]
    if joined:
        rank = lax.axis_index("dp")
        row = rank - (rank // 2) * 2
        first = pl.multiple_of((block_of((PAIR, SAME)) - row) * width, HD)
        copy = pltpu.make_async_copy(
            features.at[:, pl.ds(first, 2 * width)], both, block_sems.at[0]
        )
        copy.start()
        block_copies = [copy, None]
        block_copies += start_features(
            features, kinds[2:], blocks.at[pl.ds(2, len(kinds) - 2)], block_sems.at[pl.ds(2, len(kinds) - 2)]
        )
    else:
        block_copies = start_features(features, kinds, blocks, block_sems)
    for copy in copies:
        copy.wait()
    lengths, rewards, q, ck, nk, cot = bufs
    attend_heads(lengths, rewards, q, ck, nk, cot=cot, rows=rows)
    cots = rows[...].T.astype(jnp.bfloat16)
    cot_half[...] = cots
    place = 0
    for out, job in zip(outs, jobs):
        first = 0
        for _, size in job:
            if block_copies[place] is not None:
                block_copies[place].wait()
            if joined and place < 2:
                place_row = 1 - row if place == 0 else row
                block = both[:, pl.ds(pl.multiple_of(place_row * width, HD), width)]
            else:
                block = blocks[place]
            out[first : first + size] = jnp.dot(
                cots[:size], block, preferred_element_type=jnp.float32
            )
            first += size
            place += 1


def begin(half, jobs, arrays, features, width):
    lengths, rewards, queries, ck, _, _ = arrays
    depth = features.shape[0]
    columns = ck.shape[2] // 2
    count = max(sum(len(job) for job in jobs), 1)
    shapes = [jax.ShapeDtypeStruct((columns, depth), jnp.bfloat16)]
    for job in jobs:
        shapes.append(jax.ShapeDtypeStruct((sum(size for _, size in job), width), jnp.float32))
    vmem = pl.BlockSpec(memory_space=pltpu.VMEM)
    return pl.pallas_call(
        functools.partial(begin_kernel, half, jobs),
        in_specs=[HBM] * 7,
        out_specs=[vmem] * len(shapes),
        out_shape=shapes,
        scratch_shapes=[pltpu.SMEM(x.shape, x.dtype) for x in arrays[:2]]
        + [pltpu.VMEM(x.shape[:2] + (x.shape[2] // 2,), x.dtype) for x in arrays[2:]]
        + [
            pltpu.VMEM((depth, columns), jnp.float32),
            pltpu.VMEM((count, depth, width), jnp.bfloat16),
            pltpu.VMEM((depth, 2 * width), jnp.bfloat16),
            pltpu.SemaphoreType.DMA((6,)),
            pltpu.SemaphoreType.DMA((count,)),
        ],
        compiler_params=WIDE,
        cost_estimate=SMALL,
        name="value_cot",
    )(*arrays, features)


def attended_kernel(*refs):
    ins, out, bufs, sems = refs[:6], refs[6], refs[7:13], refs[13]
    for copy in copy_all(ins, bufs, sems):
        copy.wait()
    lengths, queries, ck, nk, cv, nv = bufs
    attend_heads(lengths, None, queries, ck, nk, cv=cv, nv=nv, out=out)


def attend(*arrays):
    queries = arrays[1]
    return pl.pallas_call(
        attended_kernel,
        in_specs=[HBM] * 6,
        out_specs=pl.BlockSpec(memory_space=pltpu.VMEM),
        out_shape=jax.ShapeDtypeStruct(queries.shape, jnp.bfloat16),
        scratch_shapes=[pltpu.SMEM(arrays[0].shape, arrays[0].dtype)]
        + [pltpu.VMEM(x.shape, x.dtype) for x in arrays[1:]]
        + [pltpu.SemaphoreType.DMA((6,))],
        compiler_params=MIDDLE,
        cost_estimate=SMALL,
        name="attend",
    )(*arrays)


def chunk_kernel(jobs, features, half_a, half_b, *refs):
    kinds = [kind for kind, _ in jobs]
    count = sum(len(which) for _, which in jobs)
    outs, (blocks, sems) = refs[:count], refs[count:]
    copies = start_features(features, kinds, blocks, sems)
    cots = (half_a, half_b)
    place = 0
    for i, (_, which) in enumerate(jobs):
        copies[i].wait()
        for h in which:
            outs[place][...] = jnp.dot(
                cots[h][...], blocks[i], preferred_element_type=jnp.float32
            )
            place += 1


def chunks(jobs, features, halves, width):
    depth = features.shape[0]
    half = halves[0].shape[0]
    count = sum(len(which) for _, which in jobs)
    vmem = pl.BlockSpec(memory_space=pltpu.VMEM)
    return pl.pallas_call(
        functools.partial(chunk_kernel, jobs),
        in_specs=[HBM, vmem, vmem],
        out_specs=[vmem] * count,
        out_shape=[jax.ShapeDtypeStruct((half, width), jnp.float32)] * count,
        scratch_shapes=[
            pltpu.VMEM((len(jobs), depth, width), jnp.bfloat16),
            pltpu.SemaphoreType.DMA((len(jobs),)),
        ],
        compiler_params=MIDDLE,
        cost_estimate=SMALL,
        name="chunk",
    )(features, *halves)


def add_kernel(*refs):
    own_a, own_b, cross, mid_a, mid_b, first, late, last_a, last_b, total, peaks = refs
    size = own_a.shape[0]
    rank = lax.axis_index("dp")
    edge = (rank < 2) | (rank >= 6)
    piece = jnp.concatenate([first[size:], late[...]], axis=0)
    arrived = jnp.where(edge, last_a[...], piece)
    total[:size] = own_a[...] + cross[:size] + mid_a[...] + arrived
    total[size:] = own_b[...] + cross[size:] + mid_b[...] + last_b[...]
    lane = lax.broadcasted_iota(jnp.int32, peaks.shape, 1)
    peak = jnp.zeros(peaks.shape, jnp.float32)
    for b in range(2 * size // BUCKET):
        top = jnp.abs(total[b * BUCKET : (b + 1) * BUCKET])
        top = jnp.max(jnp.max(top, axis=0, keepdims=True), axis=1, keepdims=True)
        peak = jnp.where(lane == b, top, peak)
    peaks[...] = peak


def add_parts(parts):
    vmem = pl.BlockSpec(memory_space=pltpu.VMEM)
    size, width = parts[0].shape
    return pl.pallas_call(
        add_kernel,
        in_specs=[vmem] * len(parts),
        out_specs=[vmem] * 2,
        out_shape=[
            jax.ShapeDtypeStruct((2 * size, width), jnp.float32),
            jax.ShapeDtypeStruct((1, HD), jnp.float32),
        ],
        compiler_params=PARAMS,
        cost_estimate=SMALL,
        name="add_parts",
    )(*parts)


def place_kernel(total, grad):
    grad[...] = total[...].T


def place(total):
    columns, width = total.shape
    vmem = pl.BlockSpec(memory_space=pltpu.VMEM)
    return pl.pallas_call(
        place_kernel,
        in_specs=[vmem],
        out_specs=vmem,
        out_shape=jax.ShapeDtypeStruct((width, columns), jnp.float32),
        compiler_params=PARAMS,
        cost_estimate=SMALL,
        name="place",
    )(total)


def reduce_on_grid(features, halves, firsts, attended, dp):
    width = features.shape[1] // dp
    columns = 2 * halves[0].shape[0]
    rank = lax.axis_index("dp")
    edge = (rank < 2) | (rank >= 6)

    def across(x):
        return lax.ppermute(x, "dp", [(r, r ^ 1) for r in range(dp)])

    def pair(x):
        return lax.ppermute(x, "dp", [(r, r ^ 2) for r in range(dp)])

    def outward(x):
        return lax.ppermute(x, "dp", [(r, r ^ 2) for r in (0, 1, 6, 7)])

    def inward(x):
        return lax.ppermute(x, "dp", [(r, r ^ 2) for r in (2, 3, 4, 5)])

    def middle(x):
        return lax.ppermute(x, "dp", [(r, r ^ 6) for r in (2, 3, 4, 5)])

    def together(*arrays):
        return lax.optimization_barrier(arrays)

    def after(x, *others):
        return together(x, *others)[0]

    def planes(x, hop):
        return lax.ppermute(x, "dp", [(r, r ^ hop) for r in range(dp)])

    def make(*jobs):
        return chunks(jobs, features, halves, width)

    a, b = 0, 1
    edge0, cross3a, cross3b = firsts
    (own3a, own3b, cross2a, cross2b, own2a, own2b, crosspb, crossoa, crossob, ownpa, ownpb, ownoa, ownob) = (
        make(
            ((FAR3, SAME), (a, b)),
            ((FAR2, CROSS), (a, b)),
            ((FAR2, SAME), (a, b)),
            ((PAIR, CROSS), (b,)),
            ((OWN, CROSS), (a, b)),
            ((PAIR, SAME), (a, b)),
            ((OWN, SAME), (a, b)),
        )
    )

    size = ownpa.shape[0]
    cut = size // EARLY
    e0 = pair(edge0)
    y0 = across(cross3a)
    y1 = after(across(cross3b), y0, e0)
    e2 = after(outward(own3a + y0), y1)
    y2 = after(across(after(cross2a, y0)), e2)
    e3 = after(outward(own3b + y1), y2)
    m3 = middle(own3a + y0 + e2)
    y3 = after(across(after(cross2b, y1, attended)), e3)
    e4 = after(outward(own2a + y2), y3)
    m4 = middle(own3b + y1 + e3)
    y4 = after(across(after(crosspb, y2)), e4)
    e5 = after(pair(jnp.where(edge, own2b + y3, ownpa + m3)), y4)
    m5 = middle(own2a + y2 + e4)
    y5 = across(after(jnp.concatenate([crossoa + e0[:size], crossob], axis=0), y3))
    late = outward(after(ownpa[cut:], m5))
    e6 = pair(ownpb + y4 + m4)
    m6 = middle(own2b + y3 + e5)
    total, peaks = add_parts([ownoa, ownob, y5, m5, m6, e0, late, e5, e6])
    grad = place(total)
    peaks = jnp.maximum(peaks, across(peaks))
    near, far, middle_peaks = [planes(peaks, hop) for hop in (2, 4, 6)]
    peaks = jnp.maximum(jnp.maximum(peaks, near), jnp.maximum(far, middle_peaks))
    return attended, grad, peaks[0, : columns // BUCKET]


def reduce_plain(features, halves):
    cots = jnp.concatenate(halves, axis=0)
    partial_grad = lax.dot_general(
        features, cots, (((0,), (1,)), ((), ())), preferred_element_type=jnp.float32
    )
    grad = lax.psum_scatter(partial_grad, "dp", scatter_dimension=0, tiled=True)
    peaks = jnp.max(jnp.abs(grad).reshape(-1, cots.shape[0] // BUCKET, BUCKET), axis=(0, 2))
    return grad, lax.pmax(peaks, "dp")


def per_device(
    dp,
    queries,
    cache_keys,
    cache_values,
    new_keys,
    new_values,
    features,
    cotangent,
    rewards,
    lengths,
):
    flat = features.reshape(-1, features.shape[2])
    arrays = (lengths, rewards, queries, cache_keys, new_keys, cotangent)
    on_grid = dp == 8
    width = features.shape[2] // 8 if on_grid else BUCKET
    half = cache_keys.shape[2] // 2
    jobs_a, jobs_b = (), ()
    if on_grid:
        jobs_a = (
            (((PAIR, CROSS), half), ((PAIR, SAME), half // EARLY)),
            (((FAR3, CROSS), half),),
        )
        jobs_b = ((((FAR3, CROSS), half),),)
    half_a, *firsts = begin(0, jobs_a, arrays, flat, width)
    half_b, *seconds = begin(1, jobs_b, arrays, flat, width)
    attended = attend(lengths, queries, cache_keys, new_keys, cache_values, new_values)
    firsts += seconds
    if on_grid:
        attended, grad, peaks = reduce_on_grid(
            flat, (half_a, half_b), firsts, attended, dp
        )
    else:
        grad, peaks = reduce_plain(flat, (half_a, half_b))
    return attended, grad, peaks


def solution(mesh):
    split = P(("groups", "dp"), None, "tensor")
    rows = P(("groups", "dp"))
    in_specs = (
        split,
        split,
        split,
        split,
        split,
        P(("groups", "dp"), None, None),
        split,
        rows,
        rows,
    )
    out_specs = (split, P(("groups", "dp"), "tensor"), P(("groups", "tensor")))
    return jax.shard_map(
        functools.partial(per_device, mesh.shape["dp"]),
        mesh=mesh,
        in_specs=in_specs,
        out_specs=out_specs,
        check_vma=False,
    )
```
